128 devices in a mesh: dp: 8 (over y, z_lo), fsdp: 16 (over z_hi, x, core).
Axes of the slice: x: 4, y: 4, z: 4 (z_hi: 2, z_lo: 2; z = z_hi * 2 + z_lo), core: 2. Of those that a mesh axis runs over, the one named last changes fastest.
Arguments:
- tokens: bfloat16 [40960, 8192], P(('dp', 'fsdp')), may hold values from -6 to 6
- master: float32 [8192, 1024], P('fsdp'), may hold values from -0.0625 to 0.0625
- previous_down_factor: float32 [8192, 512], P('fsdp'), may hold values from -0.0625 to 0.0625
- previous_up_factor: float32 [512, 1024], P('fsdp'), may hold values from -0.25 to 0.25
- fresh_down: float32 [8192, 512], P('fsdp'), may hold values from -0.0625 to 0.0625
- fresh_up: float32 [512, 1024], P('fsdp'), may hold values from -0.25 to 0.25
- cotangent: bfloat16 [40960, 1024], P(('dp', 'fsdp')), may hold values from -6 to 6
Outputs:
- merged: float32 [8192, 1024], P('fsdp')
- values: bfloat16 [40960, 1024], P(('dp', 'fsdp'))
- input_gradient: bfloat16 [40960, 8192], P(('dp', 'fsdp'))
- down_factor_gradient: float32 [8192, 512], P('fsdp')
- up_factor_gradient: float32 [512, 1024], P('fsdp')
The draws below stay inside these ranges and needn't reach their ends.
All inputs are finite; a program needn't handle non-finite values.
Results may differ from the reference program's by a relative error of at most 0.0051.
Values may be sent and summed in bfloat16 or wider, within the bound.
No kernel may reach another device: no remote copies, remote signals or barrier semaphores. Data moves between devices by JAX's collectives and lax.ppermute only.
A program may use at most 128 MiB of HBM per device.

```python
import jax
import jax.numpy as jnp
from jax import lax

D = 8192
KVW = 1024
R = 512
TOKENS = 40960


def shard_levels(rng, dims, split, low, top_value):
    loudness, own = 1.0, jax.random.fold_in(rng, 6)
    for position, shards_of in split:
        heights = jnp.exp(jax.random.uniform(jax.random.fold_in(own, position), (shards_of,), jnp.float32, low / len(split), top_value / len(split)))
        loudness = loudness * jnp.repeat(heights, dims[position] // shards_of).reshape([-1 if axis == position else 1 for axis in range(len(dims))])
    return loudness


def gaussian(rng, shape, scale, bound, split=(), held_as=jnp.bfloat16):
    entries = scale * jax.random.normal(rng, shape, jnp.float32)
    if split:
        entries = entries * shard_levels(rng, shape, split, -0.22, 0.18)
    return jnp.clip(entries, -bound, bound).astype(held_as)


def setup_inputs(seed: int = 0) -> dict:
    arg_keys = jax.random.split(jax.random.key(seed), 8)
    return {
        "tokens": gaussian(arg_keys[0], (TOKENS, D), 1.0, 6.0, ((0, 128),)),
        "master": gaussian(arg_keys[1], (D, KVW), D ** -0.5, 0.0625, ((0, 16),), jnp.float32),
        "previous_down_factor": gaussian(arg_keys[2], (D, R), D ** -0.5, 0.0625, ((0, 16),), jnp.float32),
        "previous_up_factor": gaussian(arg_keys[3], (R, KVW), R ** -0.5, 0.25, ((0, 16),), jnp.float32),
        "fresh_down": gaussian(arg_keys[4], (D, R), D ** -0.5, 0.0625, ((0, 16),), jnp.float32),
        "fresh_up": gaussian(arg_keys[5], (R, KVW), R ** -0.5, 0.25, ((0, 16),), jnp.float32),
        "cotangent": gaussian(arg_keys[6], (TOKENS, KVW), 1.0, 6.0, ((0, 128),)),
    }


adapter_scale = 0.25


def reference(tokens, master, previous_down_factor, previous_up_factor, fresh_down, fresh_up, cotangent):
    merged = master + adapter_scale * jnp.dot(previous_down_factor, previous_up_factor, precision=lax.Precision.HIGHEST, preferred_element_type=jnp.float32)
    weight_reduced_float = merged.astype(jnp.bfloat16)
    down_reduced_float = fresh_down.astype(jnp.bfloat16)
    up_reduced_float = fresh_up.astype(jnp.bfloat16)
    reduced_rank = jnp.dot(tokens, down_reduced_float, preferred_element_type=jnp.float32).astype(jnp.bfloat16)
    values = (jnp.dot(tokens, weight_reduced_float, preferred_element_type=jnp.float32) + adapter_scale * jnp.dot(reduced_rank, up_reduced_float, preferred_element_type=jnp.float32)).astype(jnp.bfloat16)
    backward_rank_rows = jnp.dot(cotangent, up_reduced_float.T, preferred_element_type=jnp.float32).astype(jnp.bfloat16)
    input_gradient = (jnp.dot(cotangent, weight_reduced_float.T, preferred_element_type=jnp.float32) + adapter_scale * jnp.dot(backward_rank_rows, down_reduced_float.T, preferred_element_type=jnp.float32)).astype(jnp.bfloat16)
    down_factor_gradient = adapter_scale * jnp.dot(tokens.T, backward_rank_rows, preferred_element_type=jnp.float32)
    up_factor_gradient = adapter_scale * jnp.dot(reduced_rank.T, cotangent, preferred_element_type=jnp.float32)
    return merged, values, input_gradient, down_factor_gradient, up_factor_gradient
```

```python
import functools

import jax
import jax.numpy as jnp
import numpy as np
from jax import lax
from jax.experimental import pallas as pl
from jax.experimental.pallas import tpu as pltpu
from jax.sharding import Mesh
from jax.sharding import PartitionSpec as P

scale = 0.25
AXES = ("y", "zl", "zh", "x", "c")
SIZES = (4, 2, 2, 4, 2)
bf16 = jnp.bfloat16
f32 = jnp.float32
VMEM = 48 * 2**20


def pairs(move):
    out = []
    for i in range(128):
        y, zl, zh, x, c = (int(v) for v in np.unravel_index(i, SIZES))
        x2, y2, z2, c2 = move(x, y, 2 * zh + zl, c)
        z2 %= 4
        j = np.ravel_multi_index((y2 % 4, z2 % 2, z2 // 2, x2 % 4, c2), SIZES)
        out.append((i, int(j)))
    return out


def sg(c):
    return 1 - 2 * c


MOVES = {
    "core": pairs(lambda x, y, z, c: (x, y, z, 1 - c)),
    "x+": pairs(lambda x, y, z, c: (x + 1, y, z, c)),
    "x-": pairs(lambda x, y, z, c: (x - 1, y, z, c)),
    "x2": pairs(lambda x, y, z, c: (x + 2, y, z, c)),
    "xp": pairs(lambda x, y, z, c: (x + sg(c), y, z, c)),
    "xq": pairs(lambda x, y, z, c: (x - sg(c), y, z, c)),
    "yp": pairs(lambda x, y, z, c: (x, y + sg(c), z, c)),
    "yq": pairs(lambda x, y, z, c: (x, y - sg(c), z, c)),
    "z1": pairs(lambda x, y, z, c: (x, y, 3 - z, c)),
    "z2": pairs(lambda x, y, z, c: (x, y, z ^ 1, c)),
}


def send(v, move):
    return lax.ppermute(v, AXES, MOVES[move])


def nt(a, b):
    return lax.dot_general(a, b, (((1,), (1,)), ((), ())), preferred_element_type=f32)


def tn(a, b):
    return lax.dot_general(a, b, (((0,), (0,)), ((), ())), preferred_element_type=f32)


def nn(a, b):
    return lax.dot_general(a, b, (((1,), (0,)), ((), ())), preferred_element_type=f32)


def pick_kernel(s_ref, t_ref, o_ref):
    o_ref[...] = t_ref[...]


def pick_columns(tokens, c):
    n, d = tokens.shape
    return pl.pallas_call(
        pick_kernel,
        grid_spec=pltpu.PrefetchScalarGridSpec(
            num_scalar_prefetch=1,
            grid=(8,),
            in_specs=[pl.BlockSpec((n, 512), lambda k, s: (0, 2 * k + 1 - s[0]))],
            out_specs=pl.BlockSpec((n, 512), lambda k, s: (0, k)),
        ),
        out_shape=jax.ShapeDtypeStruct((n, d // 2), bf16),
        name="pick_columns",
    )(c[None], tokens)


def down_kernel(s_ref, t_ref, tr_ref, br_ref, own_ref, a_ref, b_ref, far_ref, blk):
    y, c = s_ref[1], s_ref[0]
    n = t_ref.shape[0]
    blk[...] = scale * (tn(t_ref[...], br_ref[:n, :]) + tn(tr_ref[...], br_ref[n:, :]))

    def rows(rel):
        start = pl.multiple_of(((y + rel) % 4) * 128, 128)
        return blk[pl.ds(start, 128), :]

    own_ref[0] = rows(0)
    a_ref[0] = rows(1 + 2 * c)
    b_ref[0] = rows(3 - 2 * c).astype(bf16)
    far_ref[0] = rows(2).astype(bf16)


def down_partials(tokens, tokens_sib, br2, c, y):
    n = tokens.shape[0]
    spec = pl.BlockSpec((1, 128, 512), lambda k, s: (k, 0, 0))
    return pl.pallas_call(
        down_kernel,
        grid_spec=pltpu.PrefetchScalarGridSpec(
            num_scalar_prefetch=1,
            grid=(8,),
            in_specs=[
                pl.BlockSpec((n, 512), lambda k, s: (0, 2 * k + s[0])),
                pl.BlockSpec((n, 512), lambda k, s: (0, k)),
                pl.BlockSpec((2 * n, 512), lambda k, s: (0, 0)),
            ],
            out_specs=[spec] * 4,
            scratch_shapes=[pltpu.VMEM((512, 512), f32)],
        ),
        out_shape=[
            jax.ShapeDtypeStruct((8, 128, 512), f32),
            jax.ShapeDtypeStruct((8, 128, 512), f32),
            jax.ShapeDtypeStruct((8, 128, 512), bf16),
            jax.ShapeDtypeStruct((8, 128, 512), bf16),
        ],
        compiler_params=pltpu.CompilerParams(vmem_limit_bytes=VMEM),
        cost_estimate=pl.CostEstimate(flops=2 * 640 * 4096 * 512, bytes_accessed=11 * 2**20, transcendentals=0),
        name="down_partials",
    )(jnp.stack([c, y]), tokens, tokens_sib, br2)


def low_kernel(units, width, s_ref, t_hbm, tr_hbm, *rest):
    n = t_hbm.shape[0]
    d_hbm = rest[: units]
    o_ref, tbuf, dbuf, sems = rest[units:]
    copies = []
    for u in range(units):
        g = pl.multiple_of(s_ref[u] * 256, 256)
        h = pl.multiple_of(s_ref[units + u] * 256, 256)
        cps = [
            pltpu.make_async_copy(t_hbm.at[:, pl.ds(g, width)], tbuf.at[u, pl.ds(0, n)], sems.at[0, u]),
            pltpu.make_async_copy(tr_hbm.at[:, pl.ds(h, width)], tbuf.at[u, pl.ds(n, n)], sems.at[1, u]),
            pltpu.make_async_copy(d_hbm[u], dbuf.at[u], sems.at[2, u]),
        ]
        for cp in cps:
            cp.start()
        copies.append(cps)
    for u in range(units):
        for cp in copies[u]:
            cp.wait()
        part = nn(tbuf[u], dbuf[u])
        if u == 0:
            o_ref[...] = part
        else:
            o_ref[...] += part


def low_partial(tokens, tokens_sib, blocks, starts):
    n = tokens.shape[0]
    units = len(blocks)
    width = blocks[0].shape[0]
    return pl.pallas_call(
        functools.partial(low_kernel, units, width),
        in_specs=[pl.BlockSpec(memory_space=pltpu.SMEM)] + [pl.BlockSpec(memory_space=pl.ANY)] * (2 + units),
        out_specs=pl.BlockSpec(memory_space=pltpu.VMEM),
        out_shape=jax.ShapeDtypeStruct((2 * n, 512), f32),
        scratch_shapes=[
            pltpu.VMEM((units, 2 * n, width), bf16),
            pltpu.VMEM((units, width, 512), bf16),
            pltpu.SemaphoreType.DMA((3, units)),
        ],
        compiler_params=pltpu.CompilerParams(vmem_limit_bytes=VMEM),
        cost_estimate=pl.CostEstimate(
            flops=2 * 2 * n * units * width * 512, bytes_accessed=units * width * 2 * (2 * n + 512) + 8 * n * 512, transcendentals=0
        ),
        name="low_partial",
    )(starts, tokens, tokens_sib, *blocks)


def main_kernel(units, width, first, s_ref, t_hbm, tr_hbm, cot_ref, br_ref, *rest):
    n = t_hbm.shape[0]
    w_hbm = rest[:units]
    d_hbm = rest[units : 2 * units]
    rest = rest[2 * units :]
    if not first:
        v_in, _ = rest[:2]
        rest = rest[2:]
    v_ref, x_hbm, o_hbm, tbuf, wbuf, dbuf, xbuf, sems, osems = rest

    def ins(u):
        g = pl.multiple_of(s_ref[u] * 256, 256)
        h = pl.multiple_of(s_ref[units + u] * 256, 256)
        return [
            pltpu.make_async_copy(t_hbm.at[:, pl.ds(g, width)], tbuf.at[u, pl.ds(0, n)], sems.at[0, u]),
            pltpu.make_async_copy(tr_hbm.at[:, pl.ds(h, width)], tbuf.at[u, pl.ds(n, n)], sems.at[1, u]),
            pltpu.make_async_copy(w_hbm[u], wbuf.at[u], sems.at[2, u]),
            pltpu.make_async_copy(d_hbm[u], dbuf.at[u], sems.at[3, u]),
        ]

    def outs(u):
        g = pl.multiple_of(s_ref[u] * 256, 256)
        o = pl.multiple_of(s_ref[2 * units + u] * 256, 256)
        return [
            pltpu.make_async_copy(xbuf.at[u, pl.ds(0, n)], x_hbm.at[:, pl.ds(g, width)], osems.at[0, u]),
            pltpu.make_async_copy(xbuf.at[u, pl.ds(n, n)], o_hbm.at[:, pl.ds(o, width)], osems.at[1, u]),
        ]

    copies = [ins(u) for u in range(units)]
    for cps in copies:
        for cp in cps:
            cp.start()
    if not first:
        v_ref[...] = v_in[...]
    for u in range(units):
        for cp in copies[u]:
            cp.wait()
        x = nt(cot_ref[...], wbuf[u]) + scale * nt(br_ref[...], dbuf[u])
        xbuf[u] = x.astype(bf16)
        for cp in outs(u):
            cp.start()
        part = nn(tbuf[u], wbuf[u])
        if first and u == 0:
            v_ref[...] = part
        else:
            v_ref[...] += part
    for u in range(units):
        for cp in outs(u):
            cp.wait()


def main_group(tokens, tokens_sib, cot2, br2, w_blocks, d_blocks, starts, carry=None):
    n, d = tokens.shape
    units = len(w_blocks)
    width = w_blocks[0].shape[0]
    first = carry is None
    vm = pl.BlockSpec(memory_space=pltpu.VMEM)
    hbm = pl.BlockSpec(memory_space=pl.ANY)
    args = [starts, tokens, tokens_sib, cot2, br2, *w_blocks, *d_blocks]
    specs = [pl.BlockSpec(memory_space=pltpu.SMEM), hbm, hbm, vm, vm] + [hbm] * (2 * units)
    aliases = {}
    if not first:
        aliases = {len(args): 0, len(args) + 1: 1}
        args += list(carry)
        specs += [vm, hbm]
    return pl.pallas_call(
        functools.partial(main_kernel, units, width, first),
        in_specs=specs,
        out_specs=[vm, hbm, hbm],
        out_shape=[
            jax.ShapeDtypeStruct((2 * n, 1024), f32),
            jax.ShapeDtypeStruct((n, d), bf16),
            jax.ShapeDtypeStruct((n, d // 4), bf16),
        ],
        scratch_shapes=[
            pltpu.VMEM((units, 2 * n, width), bf16),
            pltpu.VMEM((units, width, 1024), bf16),
            pltpu.VMEM((units, width, 512), bf16),
            pltpu.VMEM((units, 2 * n, width), bf16),
            pltpu.SemaphoreType.DMA((4, units)),
            pltpu.SemaphoreType.DMA((2, units)),
        ],
        input_output_aliases=aliases,
        compiler_params=pltpu.CompilerParams(vmem_limit_bytes=VMEM),
        cost_estimate=pl.CostEstimate(
            flops=2 * 2 * n * units * width * 2560, bytes_accessed=24 * 2**20, transcendentals=0
        ),
        name="main_group",
    )(*args)


def place_kernel(s_ref, r_ref, x_in, x_ref):
    x_ref[...] = r_ref[...]


def place_columns(x, recv, zc):
    n, d = x.shape
    return pl.pallas_call(
        place_kernel,
        grid_spec=pltpu.PrefetchScalarGridSpec(
            num_scalar_prefetch=1,
            grid=(4,),
            in_specs=[
                pl.BlockSpec((n, 512), lambda k, s: (0, k)),
                pl.BlockSpec(memory_space=pl.ANY),
            ],
            out_specs=pl.BlockSpec((n, 512), lambda k, s: (0, s[0] * 8 + 2 * k + 1 - s[1])),
        ),
        out_shape=jax.ShapeDtypeStruct((n, d), bf16),
        input_output_aliases={2: 0},
        name="place_columns",
    )(zc, recv, x)


def gather_small(v, zh, x, c):
    other = send(v, "z1")
    both = jnp.where(zh == 0, jnp.stack([v, other]), jnp.stack([other, v]))
    ring = [both, send(both, "x-"), send(both, "x2"), send(both, "x+")]
    ring = jnp.stack(ring + ring[:3])
    half = lax.dynamic_slice_in_dim(ring, (4 - x) % 4, 4, 0)
    sib = send(half, "core")
    whole = jnp.where(c == 0, jnp.stack([half, sib], 2), jnp.stack([sib, half], 2))
    return whole.transpose(1, 0, 2, 3, 4).reshape(16 * v.shape[0], v.shape[1])


def gather_x(v):
    p = send(v, "xp")
    q = send(v, "xq")
    r = send(p, "xp")
    return [v, p, q, r]


def gather_z(blocks, zl):
    first, second = [], []
    for b in blocks:
        h = b.shape[0] // 2
        part = lax.dynamic_slice_in_dim(b, (1 - zl) * h, h, 0)
        got = send(part, "z1")
        first.append(got)
        second.append(send(got, "z2"))
    return first + second


def shards(tokens, master, prev_down, prev_up, fresh_down, fresh_up, cot):
    y, zl, zh, x, c = (lax.axis_index(a) for a in AXES)
    n = tokens.shape[0]
    up_half = fresh_up.astype(bf16)
    down_half = fresh_down.astype(bf16)

    up = gather_small(up_half, zh, x, c)
    prior = gather_small(prev_up, zh, x, c)
    tokens_sib = send(pick_columns(tokens, c), "core")
    cot2 = jnp.concatenate([cot, send(cot, "core")], 0)

    s = 1 - 2 * c
    xs = jnp.stack([x, (x - s) % 4, (x + s) % 4, (x + 2) % 4])
    near = zh * 4 + xs
    near_starts = jnp.concatenate([4 * near + 2 * c, 2 * near, 2 * xs]).astype(jnp.int32)
    far = (1 - zh) * 4 + xs
    far2 = jnp.concatenate([2 * far + zl, 2 * far + 1 - zl])
    far_c = jnp.concatenate([far, far])
    far_h = far2 - 2 * far_c
    far_starts = jnp.concatenate(
        [4 * far_c + 2 * c + far_h, far2, 2 * jnp.concatenate([xs, xs]) + far_h]
    ).astype(jnp.int32)

    d_near = gather_x(down_half)
    d_far = gather_z(d_near, zl)

    merged = master + scale * jnp.dot(
        prev_down, prior, precision=lax.Precision.HIGHEST, preferred_element_type=f32
    )
    weight = merged.astype(bf16)
    w_near = gather_x(weight)
    w_far = gather_z(w_near, zl)

    br2 = nt(cot2, up).astype(bf16)
    g_own, g_a, g_b, g_far = down_partials(tokens, tokens_sib, br2, c, y)
    from_b = send(g_b, "yq")
    relay = (g_a + send(g_far, "yp").astype(f32)).astype(bf16)
    from_a = send(relay, "yp")
    part = (g_own + from_a.astype(f32) + from_b.astype(f32)).astype(bf16)
    part = part.reshape(16, 64, 512)
    part = lax.all_to_all(part, ("zh", "x", "zl"), split_axis=0, concat_axis=0)
    down_piece = jnp.sum(part.astype(f32), 0)

    low_mine = low_partial(tokens, tokens_sib, d_near, near_starts) + low_partial(
        tokens, tokens_sib, d_far, far_starts
    )
    low_sib = send(low_mine, "core")
    low2 = (low_mine + jnp.concatenate([low_sib[n:], low_sib[:n]], 0)).astype(bf16)
    low_up = scale * nn(low2[:n], up)
    up_grad = scale * tn(low2, cot2)
    mine = lax.dynamic_index_in_dim(up_grad.reshape(8, 2, 32, 1024), c, 1, keepdims=False)
    mine = mine.reshape(8, 32, 8, 128).transpose(2, 0, 1, 3).reshape(4, 2, 8, 32, 128)
    mine = mine.reshape(64, 32, 128)
    mine = lax.all_to_all(mine, ("y", "zl", "zh", "x"), split_axis=0, concat_axis=0)
    up_piece = jnp.sum(mine, 0)

    pieces = jnp.concatenate([down_piece, up_piece.reshape(8, 512)], 0)
    pieces = jnp.broadcast_to(pieces[None], (8,) + pieces.shape)
    pieces = lax.all_to_all(pieces, ("y", "zl"), split_axis=0, concat_axis=0)
    down_grad = pieces[:, :64].reshape(512, 512)
    up_grad = pieces[:, 64:].reshape(8, 32, 128).transpose(1, 0, 2).reshape(32, 1024)

    v1, x1, o1 = main_group(tokens, tokens_sib, cot2, br2, w_near, d_near, near_starts)
    v2, x2, o2 = main_group(tokens, tokens_sib, cot2, br2, w_far, d_far, far_starts, (v1, x1))
    r1 = send(o1, "core")
    r2 = send(o2, "core")
    vr = send(v2[n:], "core")
    values = (v2[:n] + vr + low_up).astype(bf16)
    x3 = place_columns(x2, r1, jnp.stack([zh, c]))
    input_gradient = place_columns(x3, r2, jnp.stack([1 - zh, c]))
    return merged, values, input_gradient, down_grad, up_grad


def solution(mesh):
    fine = Mesh(mesh.devices.reshape(SIZES), AXES)
    dp, fsdp = ("y", "zl"), ("zh", "x", "c")
    rows, owned = P(dp + fsdp, None), P(fsdp, None)
    return jax.shard_map(
        shards,
        mesh=fine,
        in_specs=(rows, owned, owned, owned, owned, owned, rows),
        out_specs=(owned, rows, rows, owned, owned),
        check_vma=False,
    )
```

```python
import functools

import jax
import jax.numpy as jnp
import numpy as np
from jax import lax
from jax.experimental import pallas as pl
from jax.experimental.pallas import tpu as pltpu
from jax.sharding import Mesh
from jax.sharding import PartitionSpec as P

scale = 0.25
AXES = ("y", "zl", "zh", "x", "c")
SIZES = (4, 2, 2, 4, 2)
bf16 = jnp.bfloat16
f32 = jnp.float32
VMEM = 32 * 2**20
MOST = 60 * 2**20
COST = pl.CostEstimate(flops=0, bytes_accessed=2**16, transcendentals=0)


def pairs(move):
    out = []
    for i in range(128):
        y, zl, zh, x, c = (int(v) for v in np.unravel_index(i, SIZES))
        x2, y2, z2, c2 = move(x, y, 2 * zh + zl, c)
        z2 %= 4
        j = np.ravel_multi_index((y2 % 4, z2 % 2, z2 // 2, x2 % 4, c2), SIZES)
        out.append((i, int(j)))
    return out


def sg(c):
    return 1 - 2 * c


MOVES = {
    "core": pairs(lambda x, y, z, c: (x, y, z, 1 - c)),
    "xp": pairs(lambda x, y, z, c: (x + sg(c), y, z, c)),
    "xq": pairs(lambda x, y, z, c: (x - sg(c), y, z, c)),
    "z1": pairs(lambda x, y, z, c: (x, y, 3 - z, c)),
}


def send(v, move):
    return lax.ppermute(v, AXES, MOVES[move])


def nt(a, b):
    return lax.dot_general(a, b, (((1,), (1,)), ((), ())), preferred_element_type=f32)


def tn(a, b):
    return lax.dot_general(a, b, (((0,), (0,)), ((), ())), preferred_element_type=f32)


def nn(a, b):
    return lax.dot_general(a, b, (((1,), (0,)), ((), ())), preferred_element_type=f32)


def call(kernel, name, args, out_shape, scratch, aliases={}):
    hbm = pl.BlockSpec(memory_space=pltpu.HBM)
    return pl.pallas_call(
        kernel,
        in_specs=[pl.BlockSpec(memory_space=pltpu.SMEM)] + [hbm] * (len(args) - 1),
        out_specs=[hbm] * len(out_shape),
        out_shape=[jax.ShapeDtypeStruct(*s) for s in out_shape],
        scratch_shapes=scratch,
        input_output_aliases=aliases,
        compiler_params=pltpu.CompilerParams(vmem_limit_bytes=MOST),
        cost_estimate=COST,
        name=name,
    )(*args)


def column(i):
    return pl.ds(pl.multiple_of(i * 512, 512), 512)


def start(copies):
    for cp in copies:
        cp.start()
    return copies


def wait(copies):
    for cp in copies:
        cp.wait()


def row_copies(own_hbm, sib_hbm, out, sems, c):
    n = own_hbm.shape[1]
    copies = []
    for j in range(8):
        own, sib = (pl.ds(pl.multiple_of((2 * j + i) * n, n), n) for i in (c, 1 - c))
        copies.append(pltpu.make_async_copy(own_hbm.at[j], out.at[own], sems.at[0, j]))
        copies.append(pltpu.make_async_copy(sib_hbm.at[j], out.at[sib], sems.at[1, j]))
    return copies


def cot_copies(cot_hbm, tr_hbm, out, sems):
    n = cot_hbm.shape[0]
    return [
        pltpu.make_async_copy(cot_hbm, out.at[pl.ds(0, n)], sems.at[0]),
        pltpu.make_async_copy(tr_hbm.at[:, pl.ds(4096, 1024)], out.at[pl.ds(n, n)], sems.at[1]),
    ]


def prepare_kernel(up_ref, down_ref, o_ref, d_ref):
    up = up_ref[...].astype(bf16)
    for k in range(8):
        o_ref[k] = up
    d_ref[...] = down_ref[...].astype(bf16)


def prepare(up, down):
    vm = pl.BlockSpec(memory_space=pltpu.VMEM)
    return pl.pallas_call(
        prepare_kernel,
        in_specs=[vm, vm],
        out_specs=[vm, vm],
        out_shape=[jax.ShapeDtypeStruct((8,) + up.shape, bf16), jax.ShapeDtypeStruct(down.shape, bf16)],
        cost_estimate=COST,
        name="prepare",
    )(up, down)


def pick_kernel(s_ref, t_hbm, cot_hbm, p_hbm, picked, psems, osems):
    c = s_ref[0]
    picks = start([pltpu.make_async_copy(cot_hbm, picked.at[:, pl.ds(4096, 1024)], psems.at[8])])
    for k in range(8):
        there = picked.at[:, pl.ds(512 * k, 512)]
        picks += start([pltpu.make_async_copy(t_hbm.at[:, column(2 * k + 1 - c)], there, psems.at[k])])
    outs = []
    for k in range(4):
        wait(picks[2 * k + 1 : 2 * k + 3])
        there = pl.ds(1024 * k, 1024)
        outs += start([pltpu.make_async_copy(picked.at[:, there], p_hbm.at[:, there], osems.at[k])])
    there = pl.ds(4096, 1024)
    wait(picks[:1])
    outs += start([pltpu.make_async_copy(picked.at[:, there], p_hbm.at[:, there], osems.at[4])])
    wait(outs)


def pick_columns(tokens, cot, place):
    n = tokens.shape[0]
    return call(
        pick_kernel,
        "pick_columns",
        (place, tokens, cot),
        [((n, 5120), bf16)],
        [pltpu.VMEM((n, 5120), bf16), pltpu.SemaphoreType.DMA((9,)), pltpu.SemaphoreType.DMA((5,))],
    )[0]


def rank_kernel(
    s_ref, t_hbm, tr_hbm, cot_hbm, up_hbm, ups_hbm, g_hbm, whole_hbm, br_hbm,
    whole, cot2, br, flip, tbuf, gbuf, usems, csems, tsems, gsems, osems,
):
    n = t_hbm.shape[0]
    c = s_ref[0]
    first = start(row_copies(up_hbm, ups_hbm, whole, usems, c) + cot_copies(cot_hbm, tr_hbm, cot2, csems))
    ins = []
    for k in range(8):
        there = pl.ds(512 * k, 512)
        ins.append(
            [
                pltpu.make_async_copy(t_hbm.at[:, column(2 * k + c)], tbuf.at[pl.ds(0, n), there], tsems.at[0, k]),
                pltpu.make_async_copy(tr_hbm.at[:, there], tbuf.at[pl.ds(n, n), there], tsems.at[1, k]),
            ]
        )
    wait(first)
    for k in range(3):
        start(ins[k])
    flip[...] = nt(whole[...], cot2[...]).astype(bf16)
    br[...] = nt(cot2[...], whole[...]).astype(bf16)
    outs = start(
        [
            pltpu.make_async_copy(whole, whole_hbm, osems.at[0]),
            pltpu.make_async_copy(br, br_hbm, osems.at[1]),
        ]
    )
    for k in range(8):
        wait(ins[k])
        if k + 3 < 8:
            start(ins[k + 3])
        gbuf[k] = (scale * nn(flip[...], tbuf[:, 512 * k : 512 * k + 512])).astype(bf16)
        outs += start(
            [
                pltpu.make_async_copy(gbuf.at[k, :, pl.ds(128 * j, 128)], g_hbm.at[j, k], gsems.at[j, k])
                for j in range(4)
            ]
        )
    wait(outs)


def rank_partials(tokens, tokens_sib, cot, up, up_sib, place):
    n = tokens.shape[0]
    return call(
        rank_kernel,
        "rank_partials",
        (place, tokens, tokens_sib, cot, up, up_sib),
        [((4, 8, 512, 128), bf16), ((512, 1024), bf16), ((2 * n, 512), bf16)],
        [
            pltpu.VMEM((512, 1024), bf16),
            pltpu.VMEM((2 * n, 1024), bf16),
            pltpu.VMEM((2 * n, 512), bf16),
            pltpu.VMEM((512, 2 * n), bf16),
            pltpu.VMEM((2 * n, 4096), bf16),
            pltpu.VMEM((8, 512, 512), bf16),
            pltpu.SemaphoreType.DMA((2, 8)),
            pltpu.SemaphoreType.DMA((2,)),
            pltpu.SemaphoreType.DMA((2, 8)),
            pltpu.SemaphoreType.DMA((4, 8)),
            pltpu.SemaphoreType.DMA((2,)),
        ],
    )


def low_kernel(s_ref, t_hbm, d_hbm, o_hbm, tbuf, dbuf, total, obuf, tsems, dsems, osem):
    ins = []
    for k in range(8):
        there = pl.ds(1024 * k, 1024)
        ins.append(
            start(
                [
                    pltpu.make_async_copy(d_hbm.at[there], dbuf.at[there], dsems.at[k]),
                    pltpu.make_async_copy(t_hbm.at[:, there], tbuf.at[:, there], tsems.at[k]),
                ]
            )
        )
    for k in range(8):
        wait(ins[k])
        part = nn(tbuf[:, 1024 * k : 1024 * k + 1024], dbuf[1024 * k : 1024 * k + 1024, :])
        total[...] = part if k == 0 else total[...] + part
    obuf[...] = total[...].astype(bf16)
    wait(start([pltpu.make_async_copy(obuf, o_hbm, osem.at[0])]))


def low_rank(tokens, down, place):
    n = tokens.shape[0]
    return call(
        low_kernel,
        "low_rank",
        (place, tokens, down),
        [((n, 512), bf16)],
        [
            pltpu.VMEM((n, 8192), bf16),
            pltpu.VMEM((8192, 512), bf16),
            pltpu.VMEM((n, 512), f32),
            pltpu.VMEM((n, 512), bf16),
            pltpu.SemaphoreType.DMA((8,)),
            pltpu.SemaphoreType.DMA((8,)),
            pltpu.SemaphoreType.DMA((1,)),
        ],
    )[0]


def owner_kernel(
    s_ref, g_hbm, low_hbm, lows_hbm, cot_hbm, tr_hbm, o_hbm, low2, cot2, gbuf, up, obuf, lsems, csems, gsems, osems
):
    n = low_hbm.shape[0]
    c = s_ref[0]
    first = start(
        [
            pltpu.make_async_copy(low_hbm, low2.at[pl.ds(0, n)], lsems.at[0]),
            pltpu.make_async_copy(lows_hbm, low2.at[pl.ds(n, n)], lsems.at[1]),
        ]
        + cot_copies(cot_hbm, tr_hbm, cot2, csems)
    )
    ins = [start([pltpu.make_async_copy(g_hbm.at[:, k], gbuf.at[k], gsems.at[k])]) for k in range(8)]
    wait(first)
    up[...] = (scale * tn(low2[...], cot2[...])).astype(bf16)
    outs = []
    for k in range(8):
        wait(ins[k])
        g = gbuf[k].astype(f32)
        g = ((g[0] + g[1]) + (g[2] + g[3])).astype(bf16)
        rows = up[pl.ds(pl.multiple_of(64 * k + 32 * c, 32), 32), :]
        for zl in range(2):
            obuf[2 * k + zl, :256] = g[256 * zl : 256 * zl + 256]
            for j in range(4):
                cols = 512 * zl + 128 * j
                obuf[2 * k + zl, 256 + 32 * j : 288 + 32 * j] = rows[:, cols : cols + 128]
        there = pl.ds(2 * k, 2)
        outs += start([pltpu.make_async_copy(obuf.at[there], o_hbm.at[there], osems.at[k])])
    wait(outs)


def owner_pieces(g, low, low_sib, cot, tokens_sib, place):
    n = low.shape[0]
    return call(
        owner_kernel,
        "owner_pieces",
        (place, g, low, low_sib, cot, tokens_sib),
        [((16, 384, 128), bf16)],
        [
            pltpu.VMEM((2 * n, 512), bf16),
            pltpu.VMEM((2 * n, 1024), bf16),
            pltpu.VMEM((8, 4, 512, 128), bf16),
            pltpu.VMEM((512, 1024), bf16),
            pltpu.VMEM((16, 384, 128), bf16),
            pltpu.SemaphoreType.DMA((2,)),
            pltpu.SemaphoreType.DMA((2,)),
            pltpu.SemaphoreType.DMA((8,)),
            pltpu.SemaphoreType.DMA((8,)),
        ],
    )[0]


def place_rows(out_ref, own_ref, sib_ref, c):
    n = own_ref.shape[1]
    for j in range(8):
        own, sib = (pl.multiple_of((2 * j + i) * n, n) for i in (c, 1 - c))
        out_ref[pl.ds(own, n), :] = own_ref[j].astype(out_ref.dtype)
        out_ref[pl.ds(sib, n), :] = sib_ref[j].astype(out_ref.dtype)


def merge_kernel(s_ref, m_ref, a_ref, b_ref, bs_ref, o_ref, w_ref, prior):
    place_rows(prior, b_ref, bs_ref, s_ref[0])
    for j in range(4):
        cols = slice(256 * j, 256 * j + 256)
        add = lax.dot_general(
            a_ref[...], prior[:, cols], (((1,), (0,)), ((), ())),
            precision=lax.Precision.HIGHEST, preferred_element_type=f32,
        )
        out = m_ref[:, cols] + scale * add
        o_ref[:, cols] = out
        w_ref[:, cols] = out.astype(bf16)


def merge(master, prev_down, prior, prior_sib, place):
    whole = pl.BlockSpec((512, 1024), lambda i: (0, 0))
    first = pl.BlockSpec((8, 32, 1024), lambda i: (0, 0, 0))
    return pl.pallas_call(
        merge_kernel,
        grid=(1,),
        in_specs=[
            pl.BlockSpec(memory_space=pltpu.SMEM),
            whole,
            pl.BlockSpec((512, 512), lambda i: (0, 0)),
            first,
            first,
        ],
        out_specs=[whole] * 2,
        out_shape=[jax.ShapeDtypeStruct((512, 1024), f32), jax.ShapeDtypeStruct((512, 1024), bf16)],
        scratch_shapes=[pltpu.VMEM((512, 1024), f32)],
        compiler_params=pltpu.CompilerParams(vmem_limit_bytes=VMEM),
        cost_estimate=COST,
        name="merge",
    )(place, master, prev_down, prior, prior_sib)


def main_kernel(units, before, s_ref, t_hbm, tr_hbm, d_hbm, cot_hbm, br_hbm, *rest):
    n = t_hbm.shape[0]
    w_hbm, rest = rest[:units], rest[units:]
    if before:
        (v_hbm, _, r_hbm), rest = rest[:3], rest[3:]
    vo_hbm, vs_hbm, x_hbm, o_hbm, cot2, br, tbuf, wbuf, dbuf, xbuf, vbuf, lbuf, rest = *rest[:12], rest[12:]
    csems, tsems, wsems, osems, vsems, rsems = rest

    def span(u):
        return pl.ds(512 * u, 512)

    late = []
    if before:
        late = [pltpu.make_async_copy(r_hbm, lbuf, rsems.at[before])]
    ins, tokens = [], []
    for u in range(units):
        ins.append(
            [
                pltpu.make_async_copy(w_hbm[u], wbuf.at[span(u)], wsems.at[0, u]),
                pltpu.make_async_copy(d_hbm.at[column(s_ref[u])], dbuf.at[u], wsems.at[1, u]),
            ]
        )
        here = t_hbm.at[:, column(s_ref[u])]
        there = tr_hbm.at[:, column(s_ref[units + u])]
        tokens.append(pltpu.make_async_copy(here, tbuf.at[pl.ds(0, n), span(u)], tsems.at[0, u]))
        tokens.append(pltpu.make_async_copy(there, tbuf.at[pl.ds(n, n), span(u)], tsems.at[1, u]))
    if before:
        late.append(pltpu.make_async_copy(v_hbm[0], vbuf.at[pl.ds(0, n)], vsems.at[0, 4]))
        late.append(pltpu.make_async_copy(v_hbm[1], vbuf.at[pl.ds(n, n)], vsems.at[1, 4]))
    first = start(cot_copies(cot_hbm, tr_hbm, cot2, csems) + [pltpu.make_async_copy(br_hbm, br, csems.at[2])])
    start(ins[0])
    wait(first)
    outs = []
    for u in range(units):
        wait(ins[u])
        if u + 1 < units:
            start(ins[u + 1])
        else:
            start(late)
        start(tokens[2 * u : 2 * u + 2])
        x = nt(cot2[...], wbuf[512 * u : 512 * u + 512, :]) + scale * nt(br[...], dbuf[u])
        xbuf[u] = x.astype(bf16)
        outs += start(
            [
                pltpu.make_async_copy(xbuf.at[u, pl.ds(0, n)], x_hbm.at[:, column(s_ref[u])], osems.at[0, u]),
                pltpu.make_async_copy(xbuf.at[u, pl.ds(n, n)], o_hbm.at[:, span(u)], osems.at[1, u]),
            ]
        )
    wait(late)
    for u in range(before):
        there = x_hbm.at[:, column(s_ref[2 * units + u])]
        outs += start([pltpu.make_async_copy(lbuf.at[:, span(u)], there, rsems.at[u])])
    wait(tokens)
    for j in range(4):
        cols = slice(256 * j, 256 * j + 256)
        there = pl.ds(256 * j, 256)
        part = nn(tbuf[...], wbuf[:, cols])
        vbuf[:, cols] = part + vbuf[:, cols] if before else part
        outs += start(
            [
                pltpu.make_async_copy(vbuf.at[pl.ds(0, n), there], vo_hbm.at[:, there], vsems.at[0, j]),
                pltpu.make_async_copy(vbuf.at[pl.ds(n, n), there], vs_hbm.at[:, there], vsems.at[1, j]),
            ]
        )
    wait(outs)


def main_group(tokens, tokens_sib, down, cot, br2, blocks, starts, before=0, carry=()):
    n, d = tokens.shape
    units = len(blocks)
    args = [starts, tokens, tokens_sib, down, cot, br2, *blocks]
    kernel = main_kernel
    aliases = {}
    if before:
        aliases = {len(args) + 2: 2}
        args += list(carry)

        def kernel(units, before, *refs):
            at = 6 + units
            refs = refs[:at] + ((refs[at], refs[at + 1]),) + refs[at + 2 :]
            main_kernel(units, before, *refs)

    return call(
        functools.partial(kernel, units, before),
        "main_group",
        args,
        [((n, 1024), f32), ((n, 1024), f32), ((n, d), bf16), ((n, 512 * units), bf16)],
        [
            pltpu.VMEM((2 * n, 1024), bf16),
            pltpu.VMEM((2 * n, 512), bf16),
            pltpu.VMEM((2 * n, 512 * units), bf16),
            pltpu.VMEM((512 * units, 1024), bf16),
            pltpu.VMEM((units, 512, 512), bf16),
            pltpu.VMEM((units, 2 * n, 512), bf16),
            pltpu.VMEM((2 * n, 1024), f32),
            pltpu.VMEM((n, 512 * max(before, 1)), bf16),
            pltpu.SemaphoreType.DMA((3,)),
            pltpu.SemaphoreType.DMA((2, units)),
            pltpu.SemaphoreType.DMA((2, units)),
            pltpu.SemaphoreType.DMA((2, units)),
            pltpu.SemaphoreType.DMA((2, 5)),
            pltpu.SemaphoreType.DMA((before + 1,)),
        ],
        aliases,
    )


def sum_kernel(in_ref, o_ref):
    total = in_ref[0].astype(f32)
    for k in range(1, 16):
        total = total + in_ref[k].astype(f32)
    down = total[:256].T
    up = total[256:]
    for k in range(8):
        o_ref[k, :128] = down
        for j in range(2):
            o_ref[k, 128 + 32 * j : 160 + 32 * j, :128] = up[64 * j : 64 * j + 32]
            o_ref[k, 128 + 32 * j : 160 + 32 * j, 128:] = up[64 * j + 32 : 64 * j + 64]


def sum_pieces(pieces):
    vm = pl.BlockSpec(memory_space=pltpu.VMEM)
    return pl.pallas_call(
        sum_kernel,
        in_specs=[vm],
        out_specs=vm,
        out_shape=jax.ShapeDtypeStruct((8, 192, 256), f32),
        compiler_params=pltpu.CompilerParams(vmem_limit_bytes=VMEM),
        cost_estimate=COST,
        name="sum_pieces",
    )(pieces)


def join_kernel(in_ref, down_ref, up_ref):
    for y in range(4):
        for zl in range(2):
            down_ref[128 * y : 128 * y + 128, 256 * zl : 256 * zl + 256] = in_ref[2 * y + zl, :128]
    for zl in range(2):
        for j in range(2):
            rows = slice(128 + 32 * j, 160 + 32 * j)
            total = in_ref[zl, rows] + in_ref[2 + zl, rows] + in_ref[4 + zl, rows] + in_ref[6 + zl, rows]
            up_ref[:, 512 * zl + 256 * j : 512 * zl + 256 * j + 256] = total


def join_pieces(pieces):
    vm = pl.BlockSpec(memory_space=pltpu.VMEM)
    return pl.pallas_call(
        join_kernel,
        in_specs=[vm],
        out_specs=[vm, vm],
        out_shape=[jax.ShapeDtypeStruct((512, 512), f32), jax.ShapeDtypeStruct((32, 1024), f32)],
        compiler_params=pltpu.CompilerParams(vmem_limit_bytes=VMEM),
        cost_estimate=COST,
        name="join_pieces",
    )(pieces)


def finish_kernel(
    s_ref, t_hbm, d_hbm, w_hbm, ws_hbm, cot_hbm, br_hbm, vo_hbm, vr_hbm, low_hbm, up_hbm, r_hbm, x_in,
    v_hbm, x_hbm, tbuf, wbuf, dbuf, xbuf, cot, br, vo, vr, low, up, vbuf, lbuf, sems, wsems, xsems, vsems,
):
    n = cot.shape[0]
    late = [pltpu.make_async_copy(r_hbm, lbuf, sems.at[0])]
    first = start(
        [
            pltpu.make_async_copy(cot_hbm, cot, sems.at[1]),
            pltpu.make_async_copy(br_hbm.at[pl.ds(0, n)], br, sems.at[2]),
        ]
    )
    ins, tokens = [], []
    for i, w in enumerate((w_hbm, ws_hbm)):
        there = pl.ds(512 * i, 512)
        ins.append(
            [
                pltpu.make_async_copy(w, wbuf.at[there], wsems.at[0, i]),
                pltpu.make_async_copy(d_hbm.at[column(s_ref[i])], dbuf.at[i], wsems.at[1, i]),
            ]
        )
        tokens.append(pltpu.make_async_copy(t_hbm.at[:, column(s_ref[i])], tbuf.at[:, there], wsems.at[2, i]))
    rest = tokens + [
        pltpu.make_async_copy(low_hbm, low, sems.at[3]),
        pltpu.make_async_copy(up_hbm, up, sems.at[4]),
        pltpu.make_async_copy(vo_hbm, vo, sems.at[5]),
        pltpu.make_async_copy(vr_hbm, vr, sems.at[6]),
    ]
    start(ins[0])
    wait(first)
    outs = []
    for i in range(2):
        wait(ins[i])
        start(late + ins[1] if i == 0 else rest)
        x = nt(cot[...], wbuf[512 * i : 512 * i + 512, :]) + scale * nt(br[...], dbuf[i])
        xbuf[i] = x.astype(bf16)
        outs += start([pltpu.make_async_copy(xbuf.at[i], x_hbm.at[:, column(s_ref[i])], xsems.at[i])])
    wait(late)
    for u in range(3):
        there = x_hbm.at[:, column(s_ref[2 + u])]
        outs += start([pltpu.make_async_copy(lbuf.at[:, pl.ds(512 * u, 512)], there, xsems.at[2 + u])])
    wait(rest)
    for j in range(4):
        cols = slice(256 * j, 256 * j + 256)
        there = pl.ds(256 * j, 256)
        v = nn(tbuf[...], wbuf[:, cols]) + scale * nn(low[...], up[:, cols])
        vbuf[:, cols] = (vo[:, cols] + vr[:, cols] + v).astype(bf16)
        outs += start([pltpu.make_async_copy(vbuf.at[:, there], v_hbm.at[:, there], vsems.at[j])])
    wait(outs)


def finish(x, recv, tokens, down, w, w_sib, cot, br2, vo, vr, low, up, starts):
    n, d = x.shape
    return call(
        finish_kernel,
        "finish",
        (starts, tokens, down, w, w_sib, cot, br2, vo, vr, low, up, recv, x),
        [((n, 1024), bf16), ((n, d), bf16)],
        [
            pltpu.VMEM((n, 1024), bf16),
            pltpu.VMEM((1024, 1024), bf16),
            pltpu.VMEM((2, 512, 512), bf16),
            pltpu.VMEM((2, n, 512), bf16),
            pltpu.VMEM((n, 1024), bf16),
            pltpu.VMEM((n, 512), bf16),
            pltpu.VMEM((n, 1024), f32),
            pltpu.VMEM((n, 1024), f32),
            pltpu.VMEM((n, 512), bf16),
            pltpu.VMEM((512, 1024), bf16),
            pltpu.VMEM((n, 1024), bf16),
            pltpu.VMEM((n, 1536), bf16),
            pltpu.SemaphoreType.DMA((7,)),
            pltpu.SemaphoreType.DMA((3, 2)),
            pltpu.SemaphoreType.DMA((5,)),
            pltpu.SemaphoreType.DMA((4,)),
        ],
        {12: 1},
    )


def shards(tokens, master, prev_down, prev_up, fresh_down, fresh_up, cot):
    y, zl, zh, x, c = (lax.axis_index(a) for a in AXES)
    bar = lax.optimization_barrier
    place = jnp.stack([c, zh, x])

    def to_owners(v, axes):
        return lax.all_to_all(v, axes, split_axis=0, concat_axis=0)

    def first_step(v):
        return send(v, "xp"), send(v, "xq"), send(v, "z1")

    def second_step(p, q, far):
        return send(p, "xp"), send(far, "xq"), send(p, "z1")

    def first_step(v):
        return send(v, "xp"), send(v, "xq"), send(v, "z1")

    def second_step(p, q, far):
        return send(p, "xp"), send(far, "xq"), send(p, "z1")

    copies, down_half = prepare(fresh_up, fresh_down)
    copies, down_half, place = bar((copies, down_half, place))
    up = to_owners(copies, ("zh", "x"))
    down = lax.all_gather(down_half, ("zh", "x", "c"), axis=0, tiled=True)
    tokens_sib = send(pick_columns(tokens, cot, place), "core")
    prior = jnp.broadcast_to(prev_up[None], (8,) + prev_up.shape)
    up, prior, tokens_sib = bar((up, prior, tokens_sib))
    up_sib = send(up, "core")

    prior = to_owners(prior, ("zh", "x"))
    g, up_rows, br2 = rank_partials(tokens, tokens_sib, cot, up, up_sib, place)
    prior, g = bar((prior, g))
    prior_sib = send(prior, "core")
    g = to_owners(g, ("y",))

    merged, w = merge(master, prev_down, prior, prior_sib, place)
    p, q, far = bar(first_step(w))
    second = second_step(p, q, far)

    def blocks_of(core):
        s = 1 - 2 * core
        p, q, r = (x - s) % 4, (x + s) % 4, (x + 2) % 4
        here, there = 4 * zh, 4 * (1 - zh)
        one = jnp.stack([here + x, here + p, here + q, there + x])
        two = jnp.stack([here + r, there + p, there + q])
        return one, two, (there + r)[None]

    own = blocks_of(c)
    sib = [2 * k + 1 - c for k in blocks_of(1 - c)]
    starts = [
        jnp.concatenate([2 * own[0] + c, own[0]]),
        jnp.concatenate([2 * own[1] + c, own[1], sib[0]]),
        jnp.concatenate([2 * own[2] + c, sib[2], sib[1]]),
    ]
    starts = [v.astype(jnp.int32) for v in starts]

    low = low_rank(tokens, down, place)
    pieces = owner_pieces(g, low, send(low, "core"), cot, tokens_sib, place)
    shared = (tokens, tokens_sib, down, cot, br2)
    pieces, p = bar((pieces, p))
    part = main_group(*shared, [w, p, q, far], starts[0])
    r, far_q, far_p, part = bar(second + (part,))

    far_r = send(far_q, "xq")
    pieces = to_owners(pieces, ("zh", "x", "zl"))
    vo, vs, dx, other = part
    part = main_group(*shared, [r, far_p, far_q], starts[1], 4, (vo, vs, dx, send(other, "core")))
    part, pieces = bar((part, sum_pieces(pieces)))

    pieces = to_owners(pieces, ("y", "zl"))
    vo, vs, dx, other = part
    values, dx = finish(
        dx, send(other, "core"), tokens, down, far_r, send(far_r, "core"), cot, br2, vo, send(vs, "core"), low, up_rows, starts[2]
    )
    down_grad, up_grad = join_pieces(pieces)
    return merged, values, dx, down_grad, up_grad


def solution(mesh):
    fine = Mesh(mesh.devices.reshape(SIZES), AXES)
    dp, fsdp = ("y", "zl"), ("zh", "x", "c")
    rows, owned = P(dp + fsdp, None), P(fsdp, None)
    return jax.shard_map(
        shards,
        mesh=fine,
        in_specs=(rows, owned, owned, owned, owned, owned, rows),
        out_specs=(owned, rows, rows, owned, owned),
        check_vma=False,
    )
```

```python
import functools

import jax
import jax.numpy as jnp
import numpy as np
from jax import lax
from jax.experimental import pallas as pl
from jax.experimental.pallas import tpu as pltpu
from jax.sharding import Mesh
from jax.sharding import PartitionSpec as P

scale = 0.25
AXES = ("y", "zl", "zh", "x", "c")
SIZES = (4, 2, 2, 4, 2)
bf16 = jnp.bfloat16
f32 = jnp.float32
VMEM = 32 * 2**20
MOST = 60 * 2**20
COST = pl.CostEstimate(flops=0, bytes_accessed=2**16, transcendentals=0)


def pairs(move):
    out = []
    for i in range(128):
        y, zl, zh, x, c = (int(v) for v in np.unravel_index(i, SIZES))
        x2, y2, z2, c2 = move(x, y, 2 * zh + zl, c)
        z2 %= 4
        j = np.ravel_multi_index((y2 % 4, z2 % 2, z2 // 2, x2 % 4, c2), SIZES)
        out.append((i, int(j)))
    return out


def sg(c):
    return 1 - 2 * c


MOVES = {
    "core": pairs(lambda x, y, z, c: (x, y, z, 1 - c)),
    "xp": pairs(lambda x, y, z, c: (x + sg(c), y, z, c)),
    "xq": pairs(lambda x, y, z, c: (x - sg(c), y, z, c)),
    "z1": pairs(lambda x, y, z, c: (x, y, 3 - z, c)),
}


def send(v, move):
    return lax.ppermute(v, AXES, MOVES[move])


def nt(a, b):
    return lax.dot_general(a, b, (((1,), (1,)), ((), ())), preferred_element_type=f32)


def tn(a, b):
    return lax.dot_general(a, b, (((0,), (0,)), ((), ())), preferred_element_type=f32)


def nn(a, b):
    return lax.dot_general(a, b, (((1,), (0,)), ((), ())), preferred_element_type=f32)


def call(kernel, name, args, out_shape, scratch, aliases={}):
    hbm = pl.BlockSpec(memory_space=pltpu.HBM)
    return pl.pallas_call(
        kernel,
        in_specs=[pl.BlockSpec(memory_space=pltpu.SMEM)] + [hbm] * (len(args) - 1),
        out_specs=[hbm] * len(out_shape),
        out_shape=[jax.ShapeDtypeStruct(*s) for s in out_shape],
        scratch_shapes=scratch,
        input_output_aliases=aliases,
        compiler_params=pltpu.CompilerParams(vmem_limit_bytes=MOST),
        cost_estimate=COST,
        name=name,
    )(*args)


def column(i):
    return pl.ds(pl.multiple_of(i * 512, 512), 512)


def start(copies):
    for cp in copies:
        cp.start()
    return copies


def wait(copies):
    for cp in copies:
        cp.wait()


def row_copies(own_hbm, sib_hbm, out, sems, c):
    n = own_hbm.shape[1]
    copies = []
    for j in range(8):
        own, sib = (pl.ds(pl.multiple_of((2 * j + i) * n, n), n) for i in (c, 1 - c))
        copies.append(pltpu.make_async_copy(own_hbm.at[j], out.at[own], sems.at[0, j]))
        copies.append(pltpu.make_async_copy(sib_hbm.at[j], out.at[sib], sems.at[1, j]))
    return copies


def cot_copies(cot_hbm, tr_hbm, out, sems):
    n = cot_hbm.shape[0]
    return [
        pltpu.make_async_copy(cot_hbm, out.at[pl.ds(0, n)], sems.at[0]),
        pltpu.make_async_copy(tr_hbm.at[:, pl.ds(4096, 1024)], out.at[pl.ds(n, n)], sems.at[1]),
    ]


def prepare_kernel(up_ref, down_ref, o_ref, d_ref):
    up = up_ref[...].astype(bf16)
    for k in range(8):
        o_ref[k] = up
    d_ref[...] = down_ref[...].astype(bf16)


def prepare(up, down):
    vm = pl.BlockSpec(memory_space=pltpu.VMEM)
    return pl.pallas_call(
        prepare_kernel,
        in_specs=[vm, vm],
        out_specs=[vm, vm],
        out_shape=[jax.ShapeDtypeStruct((8,) + up.shape, bf16), jax.ShapeDtypeStruct(down.shape, bf16)],
        cost_estimate=COST,
        name="prepare",
    )(up, down)


def pick_kernel(s_ref, t_hbm, cot_hbm, p_hbm, picked, psems, osems):
    c = s_ref[0]
    picks = start([pltpu.make_async_copy(cot_hbm, picked.at[:, pl.ds(4096, 1024)], psems.at[8])])
    for k in range(8):
        there = picked.at[:, pl.ds(512 * k, 512)]
        picks += start([pltpu.make_async_copy(t_hbm.at[:, column(2 * k + 1 - c)], there, psems.at[k])])
    outs = []
    for k in range(4):
        wait(picks[2 * k + 1 : 2 * k + 3])
        there = pl.ds(1024 * k, 1024)
        outs += start([pltpu.make_async_copy(picked.at[:, there], p_hbm.at[:, there], osems.at[k])])
    there = pl.ds(4096, 1024)
    wait(picks[:1])
    outs += start([pltpu.make_async_copy(picked.at[:, there], p_hbm.at[:, there], osems.at[4])])
    wait(outs)


def pick_columns(tokens, cot, place):
    n = tokens.shape[0]
    return call(
        pick_kernel,
        "pick_columns",
        (place, tokens, cot),
        [((n, 5120), bf16)],
        [pltpu.VMEM((n, 5120), bf16), pltpu.SemaphoreType.DMA((9,)), pltpu.SemaphoreType.DMA((5,))],
    )[0]


def rank_kernel(
    s_ref, t_hbm, tr_hbm, cot_hbm, up_hbm, ups_hbm, g_hbm, whole_hbm, br_hbm,
    whole, cot2, br, flip, tbuf, gbuf, usems, csems, tsems, gsems, osems,
):
    n = t_hbm.shape[0]
    c = s_ref[0]
    first = start(row_copies(up_hbm, ups_hbm, whole, usems, c) + cot_copies(cot_hbm, tr_hbm, cot2, csems))
    ins = []
    for k in range(8):
        there = pl.ds(512 * k, 512)
        ins.append(
            [
                pltpu.make_async_copy(t_hbm.at[:, column(2 * k + c)], tbuf.at[pl.ds(0, n), there], tsems.at[0, k]),
                pltpu.make_async_copy(tr_hbm.at[:, there], tbuf.at[pl.ds(n, n), there], tsems.at[1, k]),
            ]
        )
    wait(first)
    for k in range(3):
        start(ins[k])
    flip[...] = nt(whole[...], cot2[...]).astype(bf16)
    br[...] = nt(cot2[...], whole[...]).astype(bf16)
    outs = start(
        [
            pltpu.make_async_copy(whole, whole_hbm, osems.at[0]),
            pltpu.make_async_copy(br, br_hbm, osems.at[1]),
        ]
    )
    for k in range(8):
        wait(ins[k])
        if k + 3 < 8:
            start(ins[k + 3])
        gbuf[k] = (scale * nn(flip[...], tbuf[:, 512 * k : 512 * k + 512])).astype(bf16)
        outs += start(
            [
                pltpu.make_async_copy(gbuf.at[k, :, pl.ds(128 * j, 128)], g_hbm.at[j, k], gsems.at[j, k])
                for j in range(4)
            ]
        )
    wait(outs)


def rank_partials(tokens, tokens_sib, cot, up, up_sib, place):
    n = tokens.shape[0]
    return call(
        rank_kernel,
        "rank_partials",
        (place, tokens, tokens_sib, cot, up, up_sib),
        [((4, 8, 512, 128), bf16), ((512, 1024), bf16), ((2 * n, 512), bf16)],
        [
            pltpu.VMEM((512, 1024), bf16),
            pltpu.VMEM((2 * n, 1024), bf16),
            pltpu.VMEM((2 * n, 512), bf16),
            pltpu.VMEM((512, 2 * n), bf16),
            pltpu.VMEM((2 * n, 4096), bf16),
            pltpu.VMEM((8, 512, 512), bf16),
            pltpu.SemaphoreType.DMA((2, 8)),
            pltpu.SemaphoreType.DMA((2,)),
            pltpu.SemaphoreType.DMA((2, 8)),
            pltpu.SemaphoreType.DMA((4, 8)),
            pltpu.SemaphoreType.DMA((2,)),
        ],
    )


def low_kernel(s_ref, t_hbm, d_hbm, o_hbm, tbuf, dbuf, total, obuf, tsems, dsems, osem):
    ins = []
    for k in range(8):
        there = pl.ds(1024 * k, 1024)
        ins.append(
            start(
                [
                    pltpu.make_async_copy(d_hbm.at[there], dbuf.at[there], dsems.at[k]),
                    pltpu.make_async_copy(t_hbm.at[:, there], tbuf.at[:, there], tsems.at[k]),
                ]
            )
        )
    for k in range(8):
        wait(ins[k])
        part = nn(tbuf[:, 1024 * k : 1024 * k + 1024], dbuf[1024 * k : 1024 * k + 1024, :])
        total[...] = part if k == 0 else total[...] + part
    obuf[...] = total[...].astype(bf16)
    wait(start([pltpu.make_async_copy(obuf, o_hbm, osem.at[0])]))


def low_rank(tokens, down, place):
    n = tokens.shape[0]
    return call(
        low_kernel,
        "low_rank",
        (place, tokens, down),
        [((n, 512), bf16)],
        [
            pltpu.VMEM((n, 8192), bf16),
            pltpu.VMEM((8192, 512), bf16),
            pltpu.VMEM((n, 512), f32),
            pltpu.VMEM((n, 512), bf16),
            pltpu.SemaphoreType.DMA((8,)),
            pltpu.SemaphoreType.DMA((8,)),
            pltpu.SemaphoreType.DMA((1,)),
        ],
    )[0]


def owner_kernel(
    s_ref, g_hbm, low_hbm, lows_hbm, cot_hbm, tr_hbm, o_hbm, low2, cot2, gbuf, up, obuf, lsems, csems, gsems, osems
):
    n = low_hbm.shape[0]
    c = s_ref[0]
    first = start(
        [
            pltpu.make_async_copy(low_hbm, low2.at[pl.ds(0, n)], lsems.at[0]),
            pltpu.make_async_copy(lows_hbm, low2.at[pl.ds(n, n)], lsems.at[1]),
        ]
        + cot_copies(cot_hbm, tr_hbm, cot2, csems)
    )
    ins = [start([pltpu.make_async_copy(g_hbm.at[:, k], gbuf.at[k], gsems.at[k])]) for k in range(8)]
    wait(first)
    up[...] = (scale * tn(low2[...], cot2[...])).astype(bf16)
    outs = []
    for k in range(8):
        wait(ins[k])
        g = gbuf[k].astype(f32)
        g = ((g[0] + g[1]) + (g[2] + g[3])).astype(bf16)
        rows = up[pl.ds(pl.multiple_of(64 * k + 32 * c, 32), 32), :]
        for zl in range(2):
            obuf[2 * k + zl, :256] = g[256 * zl : 256 * zl + 256]
            for j in range(4):
                cols = 512 * zl + 128 * j
                obuf[2 * k + zl, 256 + 32 * j : 288 + 32 * j] = rows[:, cols : cols + 128]
        there = pl.ds(2 * k, 2)
        outs += start([pltpu.make_async_copy(obuf.at[there], o_hbm.at[there], osems.at[k])])
    wait(outs)


def owner_pieces(g, low, low_sib, cot, tokens_sib, place):
    n = low.shape[0]
    return call(
        owner_kernel,
        "owner_pieces",
        (place, g, low, low_sib, cot, tokens_sib),
        [((16, 384, 128), bf16)],
        [
            pltpu.VMEM((2 * n, 512), bf16),
            pltpu.VMEM((2 * n, 1024), bf16),
            pltpu.VMEM((8, 4, 512, 128), bf16),
            pltpu.VMEM((512, 1024), bf16),
            pltpu.VMEM((16, 384, 128), bf16),
            pltpu.SemaphoreType.DMA((2,)),
            pltpu.SemaphoreType.DMA((2,)),
            pltpu.SemaphoreType.DMA((8,)),
            pltpu.SemaphoreType.DMA((8,)),
        ],
    )[0]


def place_rows(out_ref, own_ref, sib_ref, c):
    n = own_ref.shape[1]
    for j in range(8):
        own, sib = (pl.multiple_of((2 * j + i) * n, n) for i in (c, 1 - c))
        out_ref[pl.ds(own, n), :] = own_ref[j].astype(out_ref.dtype)
        out_ref[pl.ds(sib, n), :] = sib_ref[j].astype(out_ref.dtype)


def merge_kernel(s_ref, m_ref, a_ref, b_ref, bs_ref, o_ref, w_ref, prior):
    place_rows(prior, b_ref, bs_ref, s_ref[0])
    for j in range(4):
        cols = slice(256 * j, 256 * j + 256)
        add = lax.dot_general(
            a_ref[...], prior[:, cols], (((1,), (0,)), ((), ())),
            precision=lax.Precision.HIGHEST, preferred_element_type=f32,
        )
        out = m_ref[:, cols] + scale * add
        o_ref[:, cols] = out
        w_ref[:, cols] = out.astype(bf16)


def merge(master, prev_down, prior, prior_sib, place):
    whole = pl.BlockSpec((512, 1024), lambda i: (0, 0))
    first = pl.BlockSpec((8, 32, 1024), lambda i: (0, 0, 0))
    return pl.pallas_call(
        merge_kernel,
        grid=(1,),
        in_specs=[
            pl.BlockSpec(memory_space=pltpu.SMEM),
            whole,
            pl.BlockSpec((512, 512), lambda i: (0, 0)),
            first,
            first,
        ],
        out_specs=[whole] * 2,
        out_shape=[jax.ShapeDtypeStruct((512, 1024), f32), jax.ShapeDtypeStruct((512, 1024), bf16)],
        scratch_shapes=[pltpu.VMEM((512, 1024), f32)],
        compiler_params=pltpu.CompilerParams(vmem_limit_bytes=VMEM),
        cost_estimate=COST,
        name="merge",
    )(place, master, prev_down, prior, prior_sib)


def main_kernel(units, before, s_ref, t_hbm, tr_hbm, d_hbm, cot_hbm, br_hbm, *rest):
    n = t_hbm.shape[0]
    w_hbm, rest = rest[:units], rest[units:]
    if before:
        (v_hbm, _, r_hbm), rest = rest[:3], rest[3:]
    vo_hbm, vs_hbm, x_hbm, o_hbm, cot2, br, tbuf, wbuf, dbuf, xbuf, vbuf, lbuf, rest = *rest[:12], rest[12:]
    csems, tsems, wsems, osems, vsems, rsems = rest

    def span(u):
        return pl.ds(512 * u, 512)

    late = []
    if before:
        late = [pltpu.make_async_copy(r_hbm, lbuf, rsems.at[before])]
    ins, tokens = [], []
    for u in range(units):
        ins.append(
            [
                pltpu.make_async_copy(w_hbm[u], wbuf.at[span(u)], wsems.at[0, u]),
                pltpu.make_async_copy(d_hbm.at[column(s_ref[2 * units + before + u])], dbuf.at[u], wsems.at[1, u]),
            ]
        )
        here = t_hbm.at[:, column(s_ref[u])]
        there = tr_hbm.at[:, column(s_ref[units + u])]
        tokens.append(pltpu.make_async_copy(here, tbuf.at[pl.ds(0, n), span(u)], tsems.at[0, u]))
        tokens.append(pltpu.make_async_copy(there, tbuf.at[pl.ds(n, n), span(u)], tsems.at[1, u]))
    if before:
        late.append(pltpu.make_async_copy(v_hbm[0], vbuf.at[pl.ds(0, n)], vsems.at[0, 4]))
        late.append(pltpu.make_async_copy(v_hbm[1], vbuf.at[pl.ds(n, n)], vsems.at[1, 4]))
    first = start(cot_copies(cot_hbm, tr_hbm, cot2, csems) + [pltpu.make_async_copy(br_hbm, br, csems.at[2])])
    start(ins[0])
    wait(first)
    outs = []
    for u in range(units):
        wait(ins[u])
        if u + 1 < units:
            start(ins[u + 1])
        else:
            start(late)
        start(tokens[2 * u : 2 * u + 2])
        x = nt(cot2[...], wbuf[512 * u : 512 * u + 512, :]) + scale * nt(br[...], dbuf[u])
        xbuf[u] = x.astype(bf16)
        outs += start(
            [
                pltpu.make_async_copy(xbuf.at[u, pl.ds(0, n)], x_hbm.at[:, column(s_ref[u])], osems.at[0, u]),
                pltpu.make_async_copy(xbuf.at[u, pl.ds(n, n)], o_hbm.at[:, span(u)], osems.at[1, u]),
            ]
        )
    wait(late)
    for u in range(before):
        there = x_hbm.at[:, column(s_ref[2 * units + u])]
        outs += start([pltpu.make_async_copy(lbuf.at[:, span(u)], there, rsems.at[u])])
    wait(tokens)
    for j in range(4):
        cols = slice(256 * j, 256 * j + 256)
        there = pl.ds(256 * j, 256)
        part = nn(tbuf[...], wbuf[:, cols])
        vbuf[:, cols] = part + vbuf[:, cols] if before else part
        outs += start(
            [
                pltpu.make_async_copy(vbuf.at[pl.ds(0, n), there], vo_hbm.at[:, there], vsems.at[0, j]),
                pltpu.make_async_copy(vbuf.at[pl.ds(n, n), there], vs_hbm.at[:, there], vsems.at[1, j]),
            ]
        )
    wait(outs)


def main_group(tokens, tokens_sib, down, cot, br2, blocks, starts, before=0, carry=()):
    n, d = tokens.shape
    units = len(blocks)
    args = [starts, tokens, tokens_sib, down, cot, br2, *blocks]
    kernel = main_kernel
    aliases = {}
    if before:
        aliases = {len(args) + 2: 2}
        args += list(carry)

        def kernel(units, before, *refs):
            at = 6 + units
            refs = refs[:at] + ((refs[at], refs[at + 1]),) + refs[at + 2 :]
            main_kernel(units, before, *refs)

    return call(
        functools.partial(kernel, units, before),
        "main_group",
        args,
        [((n, 1024), f32), ((n, 1024), f32), ((n, d), bf16), ((n, 512 * units), bf16)],
        [
            pltpu.VMEM((2 * n, 1024), bf16),
            pltpu.VMEM((2 * n, 512), bf16),
            pltpu.VMEM((2 * n, 512 * units), bf16),
            pltpu.VMEM((512 * units, 1024), bf16),
            pltpu.VMEM((units, 512, 512), bf16),
            pltpu.VMEM((units, 2 * n, 512), bf16),
            pltpu.VMEM((2 * n, 1024), f32),
            pltpu.VMEM((n, 512 * max(before, 1)), bf16),
            pltpu.SemaphoreType.DMA((3,)),
            pltpu.SemaphoreType.DMA((2, units)),
            pltpu.SemaphoreType.DMA((2, units)),
            pltpu.SemaphoreType.DMA((2, units)),
            pltpu.SemaphoreType.DMA((2, 5)),
            pltpu.SemaphoreType.DMA((before + 1,)),
        ],
        aliases,
    )


def sum_kernel(in_ref, o_ref):
    total = in_ref[0].astype(f32)
    for k in range(1, 16):
        total = total + in_ref[k].astype(f32)
    down = total[:256].T.astype(bf16)
    up = total[256:].astype(bf16)
    for k in range(8):
        o_ref[k, :128] = down
        for j in range(2):
            o_ref[k, 128 + 32 * j : 160 + 32 * j, :128] = up[64 * j : 64 * j + 32]
            o_ref[k, 128 + 32 * j : 160 + 32 * j, 128:] = up[64 * j + 32 : 64 * j + 64]


def sum_pieces(pieces):
    vm = pl.BlockSpec(memory_space=pltpu.VMEM)
    return pl.pallas_call(
        sum_kernel,
        in_specs=[vm],
        out_specs=vm,
        out_shape=jax.ShapeDtypeStruct((8, 192, 256), bf16),
        compiler_params=pltpu.CompilerParams(vmem_limit_bytes=VMEM),
        cost_estimate=COST,
        name="sum_pieces",
    )(pieces)


def join_kernel(in_ref, down_ref, up_ref):
    for y in range(4):
        for zl in range(2):
            there = slice(256 * zl, 256 * zl + 256)
            down_ref[128 * y : 128 * y + 128, there] = in_ref[2 * y + zl, :128].astype(f32)
    for zl in range(2):
        for j in range(2):
            rows = slice(128 + 32 * j, 160 + 32 * j)
            parts = [in_ref[2 * y + zl, rows].astype(f32) for y in range(4)]
            total = (parts[0] + parts[1]) + (parts[2] + parts[3])
            up_ref[:, 512 * zl + 256 * j : 512 * zl + 256 * j + 256] = total


def join_pieces(pieces):
    vm = pl.BlockSpec(memory_space=pltpu.VMEM)
    return pl.pallas_call(
        join_kernel,
        in_specs=[vm],
        out_specs=[vm, vm],
        out_shape=[jax.ShapeDtypeStruct((512, 512), f32), jax.ShapeDtypeStruct((32, 1024), f32)],
        compiler_params=pltpu.CompilerParams(vmem_limit_bytes=VMEM),
        cost_estimate=COST,
        name="join_pieces",
    )(pieces)


def place_kernel(s_ref, r_hbm, vo_hbm, vr_hbm, low_hbm, up_hbm, x_in, v_hbm, x_hbm, rbuf, vo, vr, low, up, sems, xsems, vsems):
    ins = start([pltpu.make_async_copy(low_hbm, low, sems.at[0]), pltpu.make_async_copy(up_hbm, up, sems.at[1])])
    late = start([pltpu.make_async_copy(r_hbm, rbuf, sems.at[2])])
    ins += start([pltpu.make_async_copy(vo_hbm, vo, sems.at[3]), pltpu.make_async_copy(vr_hbm, vr, sems.at[4])])
    wait(late)
    outs = []
    for u in range(4):
        there = x_hbm.at[:, column(s_ref[u])]
        outs += start([pltpu.make_async_copy(rbuf.at[:, pl.ds(512 * u, 512)], there, xsems.at[u])])
    wait(ins)
    for j in range(4):
        cols = slice(256 * j, 256 * j + 256)
        there = pl.ds(256 * j, 256)
        vo[:, cols] = vo[:, cols] + vr[:, cols] + scale * nn(low[...], up[:, cols])
        outs += start([pltpu.make_async_copy(vo.at[:, there], v_hbm.at[:, there], vsems.at[j])])
    wait(outs)


def place_columns(x, recv, vo, vr, low, up, starts):
    n, d = x.shape
    return call(
        place_kernel,
        "place_columns",
        (starts, recv, vo, vr, low, up, x),
        [((n, 1024), f32), ((n, d), bf16)],
        [
            pltpu.VMEM((n, 2048), bf16),
            pltpu.VMEM((n, 1024), f32),
            pltpu.VMEM((n, 1024), f32),
            pltpu.VMEM((n, 512), bf16),
            pltpu.VMEM((512, 1024), bf16),
            pltpu.SemaphoreType.DMA((5,)),
            pltpu.SemaphoreType.DMA((4,)),
            pltpu.SemaphoreType.DMA((4,)),
        ],
        {6: 1},
    )


def finish_kernel(
    s_ref, t_hbm, d_hbm, w_hbm, ws_hbm, cot_hbm, br_hbm, vs_hbm, x_in,
    v_hbm, x_hbm, tbuf, wbuf, dbuf, xbuf, cot, br, vs, vbuf, sems, wsems, xsems, vsems,
):
    n = cot.shape[0]
    first = start(
        [
            pltpu.make_async_copy(cot_hbm, cot, sems.at[1]),
            pltpu.make_async_copy(br_hbm.at[pl.ds(0, n)], br, sems.at[2]),
        ]
    )
    ins, rest = [], []
    for i, w in enumerate((w_hbm, ws_hbm)):
        there = pl.ds(512 * i, 512)
        ins.append(
            [
                pltpu.make_async_copy(w, wbuf.at[there], wsems.at[0, i]),
                pltpu.make_async_copy(d_hbm.at[column(s_ref[i])], dbuf.at[i], wsems.at[1, i]),
            ]
        )
        rest.append(pltpu.make_async_copy(t_hbm.at[:, column(s_ref[i])], tbuf.at[:, there], wsems.at[2, i]))
    rest.append(pltpu.make_async_copy(vs_hbm, vs, sems.at[0]))
    start(ins[0])
    wait(first)
    outs = []
    for i in range(2):
        wait(ins[i])
        start(ins[1] if i == 0 else rest)
        x = nt(cot[...], wbuf[512 * i : 512 * i + 512, :]) + scale * nt(br[...], dbuf[i])
        xbuf[i] = x.astype(bf16)
        outs += start([pltpu.make_async_copy(xbuf.at[i], x_hbm.at[:, column(s_ref[i])], xsems.at[i])])
    wait(rest)
    for j in range(4):
        cols = slice(256 * j, 256 * j + 256)
        there = pl.ds(256 * j, 256)
        vbuf[:, cols] = (vs[:, cols] + nn(tbuf[...], wbuf[:, cols])).astype(bf16)
        outs += start([pltpu.make_async_copy(vbuf.at[:, there], v_hbm.at[:, there], vsems.at[j])])
    wait(outs)


def finish(x, tokens, down, w, w_sib, cot, br2, vs, starts):
    n, d = x.shape
    return call(
        finish_kernel,
        "finish",
        (starts, tokens, down, w, w_sib, cot, br2, vs, x),
        [((n, 1024), bf16), ((n, d), bf16)],
        [
            pltpu.VMEM((n, 1024), bf16),
            pltpu.VMEM((1024, 1024), bf16),
            pltpu.VMEM((2, 512, 512), bf16),
            pltpu.VMEM((2, n, 512), bf16),
            pltpu.VMEM((n, 1024), bf16),
            pltpu.VMEM((n, 512), bf16),
            pltpu.VMEM((n, 1024), f32),
            pltpu.VMEM((n, 1024), bf16),
            pltpu.SemaphoreType.DMA((3,)),
            pltpu.SemaphoreType.DMA((3, 2)),
            pltpu.SemaphoreType.DMA((2,)),
            pltpu.SemaphoreType.DMA((4,)),
        ],
        {8: 1},
    )


def shards(tokens, master, prev_down, prev_up, fresh_down, fresh_up, cot):
    y, zl, zh, x, c = (lax.axis_index(a) for a in AXES)
    bar = lax.optimization_barrier
    place = jnp.stack([c, zh, x])

    def to_owners(v, axes):
        return lax.all_to_all(v, axes, split_axis=0, concat_axis=0)

    def first_step(v):
        return send(v, "xp"), send(v, "xq"), send(v, "z1")

    def second_step(p, q, far):
        return send(p, "xp"), send(far, "xq"), send(p, "z1")

    def first_step(v):
        return send(v, "xp"), send(v, "xq"), send(v, "z1")

    def second_step(p, q, far):
        return send(p, "xp"), send(far, "xq"), send(p, "z1")

    copies, down_half = prepare(fresh_up, fresh_down)
    copies, down_half, place = bar((copies, down_half, place))
    up = to_owners(copies, ("zh", "x"))
    down = lax.all_gather(down_half, ("zh", "x", "c"), axis=0, tiled=True)
    picked = pick_columns(tokens, cot, place)
    prior = jnp.broadcast_to(prev_up[None], (8,) + prev_up.shape)
    up, prior, picked = bar((up, prior, picked))
    tokens_sib = send(picked, "core")
    up_sib = send(up, "core")

    prior = to_owners(prior, ("zh", "x"))
    g, up_rows, br2 = rank_partials(tokens, tokens_sib, cot, up, up_sib, place)
    prior, g = bar((prior, g))
    prior_sib = send(prior, "core")
    g = to_owners(g, ("y",))

    merged, w = merge(master, prev_down, prior, prior_sib, place)
    first = first_step(w)

    def groups_of(core):
        s = 1 - 2 * core
        p, q, r = (x - s) % 4, (x + s) % 4, (x + 2) % 4
        here, there = 4 * zh, 4 * (1 - zh)
        own, two = (here + x)[None], jnp.stack([here + p, here + q])
        four = jnp.stack([there + x, here + r, there + p, there + q])
        return own, two, four, (there + r)[None]

    own = groups_of(c)
    mine = [2 * k + c for k in own]
    sib = [2 * k + 1 - c for k in groups_of(1 - c)]
    starts = [
        jnp.concatenate([mine[0], own[0], 0 * own[0]]),
        jnp.concatenate([mine[1], own[1], sib[0], mine[1]]),
        jnp.concatenate([mine[2], own[2], sib[1], mine[2]]),
        sib[2],
        jnp.concatenate([mine[3], sib[3]]),
    ]
    starts = [v.astype(jnp.int32) for v in starts]

    vo, vs, dx, other = main_group(tokens, tokens_sib, down_half, cot, br2, [w], starts[0])
    p, q, far, vo, vs, dx, other = bar(first + (vo, vs, dx, other))
    second = second_step(p, q, far)

    shared = (tokens, tokens_sib, down, cot, br2)
    low = low_rank(tokens, down, place)
    pieces = owner_pieces(g, low, send(low, "core"), cot, tokens_sib, place)
    pieces, p = bar((pieces, p))
    part = main_group(*shared, [p, q], starts[1], 1, (vo, vs, dx, send(other, "core")))
    r, far_q, far_p, part = bar(second + (part,))

    far_r = send(far_q, "xq")
    pieces = to_owners(pieces, ("zh", "x", "zl"))
    vo, vs, dx, other = part
    part = main_group(*shared, [far, r, far_p, far_q], starts[2], 2, (vo, vs, dx, send(other, "core")))
    part, pieces = bar((part, sum_pieces(pieces)))

    pieces = to_owners(pieces, ("y", "zl"))
    vo, vs, dx, other = part
    v, dx = place_columns(dx, send(other, "core"), vo, send(vs, "core"), low, up_rows, starts[3])
    values, dx = finish(dx, tokens, down, far_r, send(far_r, "core"), cot, br2, v, starts[4])
    pieces, values = bar((pieces, values))
    down_grad, up_grad = join_pieces(pieces)
    return merged, values, dx, down_grad, up_grad


def solution(mesh):
    fine = Mesh(mesh.devices.reshape(SIZES), AXES)
    dp, fsdp = ("y", "zl"), ("zh", "x", "c")
    rows, owned = P(dp + fsdp, None), P(fsdp, None)
    return jax.shard_map(
        shards,
        mesh=fine,
        in_specs=(rows, owned, owned, owned, owned, owned, rows),
        out_specs=(owned, rows, rows, owned, owned),
        check_vma=False,
    )
```

```python
import functools

import jax
import jax.numpy as jnp
import numpy as np
from jax import lax
from jax.experimental import pallas as pl
from jax.experimental.pallas import tpu as pltpu
from jax.sharding import Mesh
from jax.sharding import PartitionSpec as P

scale = 0.25
AXES = ("y", "zl", "zh", "x", "c")
SIZES = (4, 2, 2, 4, 2)
bf16 = jnp.bfloat16
f32 = jnp.float32
VMEM = 32 * 2**20
MOST = 60 * 2**20
COST = pl.CostEstimate(flops=0, bytes_accessed=2**16, transcendentals=0)


def pairs(move):
    out = []
    for i in range(128):
        y, zl, zh, x, c = (int(v) for v in np.unravel_index(i, SIZES))
        x2, y2, z2, c2 = move(x, y, 2 * zh + zl, c)
        z2 %= 4
        j = np.ravel_multi_index((y2 % 4, z2 % 2, z2 // 2, x2 % 4, c2), SIZES)
        out.append((i, int(j)))
    return out


def sg(c):
    return 1 - 2 * c


MOVES = {
    "core": pairs(lambda x, y, z, c: (x, y, z, 1 - c)),
    "xp": pairs(lambda x, y, z, c: (x + sg(c), y, z, c)),
    "xq": pairs(lambda x, y, z, c: (x - sg(c), y, z, c)),
    "z1": pairs(lambda x, y, z, c: (x, y, 3 - z, c)),
}


def send(v, move):
    return lax.ppermute(v, AXES, MOVES[move])


def nt(a, b):
    return lax.dot_general(a, b, (((1,), (1,)), ((), ())), preferred_element_type=f32)


def tn(a, b):
    return lax.dot_general(a, b, (((0,), (0,)), ((), ())), preferred_element_type=f32)


def nn(a, b):
    return lax.dot_general(a, b, (((1,), (0,)), ((), ())), preferred_element_type=f32)


def call(kernel, name, args, out_shape, scratch, aliases={}):
    hbm = pl.BlockSpec(memory_space=pltpu.HBM)
    return pl.pallas_call(
        kernel,
        in_specs=[pl.BlockSpec(memory_space=pltpu.SMEM)] + [hbm] * (len(args) - 1),
        out_specs=[hbm] * len(out_shape),
        out_shape=[jax.ShapeDtypeStruct(*s) for s in out_shape],
        scratch_shapes=scratch,
        input_output_aliases=aliases,
        compiler_params=pltpu.CompilerParams(vmem_limit_bytes=MOST),
        cost_estimate=COST,
        name=name,
    )(*args)


def column(i):
    return pl.ds(pl.multiple_of(i * 512, 512), 512)


def start(copies):
    for cp in copies:
        cp.start()
    return copies


def wait(copies):
    for cp in copies:
        cp.wait()


def row_copies(own_hbm, sib_hbm, out, sems, c):
    n = own_hbm.shape[1]
    copies = []
    for j in range(8):
        own, sib = (pl.ds(pl.multiple_of((2 * j + i) * n, n), n) for i in (c, 1 - c))
        copies.append(pltpu.make_async_copy(own_hbm.at[j], out.at[own], sems.at[0, j]))
        copies.append(pltpu.make_async_copy(sib_hbm.at[j], out.at[sib], sems.at[1, j]))
    return copies


def cot_copies(cot_hbm, tr_hbm, out, sems):
    n = cot_hbm.shape[0]
    return [
        pltpu.make_async_copy(cot_hbm, out.at[pl.ds(0, n)], sems.at[0]),
        pltpu.make_async_copy(tr_hbm.at[:, pl.ds(4096, 1024)], out.at[pl.ds(n, n)], sems.at[1]),
    ]


def prepare_kernel(up_ref, down_ref, o_ref, d_ref):
    up = up_ref[...].astype(bf16)
    for k in range(8):
        o_ref[k] = up
    d_ref[...] = down_ref[...].astype(bf16)


def prepare(up, down):
    vm = pl.BlockSpec(memory_space=pltpu.VMEM)
    return pl.pallas_call(
        prepare_kernel,
        in_specs=[vm, vm],
        out_specs=[vm, vm],
        out_shape=[jax.ShapeDtypeStruct((8,) + up.shape, bf16), jax.ShapeDtypeStruct(down.shape, bf16)],
        cost_estimate=COST,
        name="prepare",
    )(up, down)


def pick_kernel(s_ref, t_hbm, cot_hbm, p_hbm, picked, psems, osems):
    c = s_ref[0]
    picks = start([pltpu.make_async_copy(cot_hbm, picked.at[:, pl.ds(4096, 1024)], psems.at[8])])
    for k in range(8):
        there = picked.at[:, pl.ds(512 * k, 512)]
        picks += start([pltpu.make_async_copy(t_hbm.at[:, column(2 * k + 1 - c)], there, psems.at[k])])
    outs = []
    for k in range(4):
        wait(picks[2 * k + 1 : 2 * k + 3])
        there = pl.ds(1024 * k, 1024)
        outs += start([pltpu.make_async_copy(picked.at[:, there], p_hbm.at[:, there], osems.at[k])])
    there = pl.ds(4096, 1024)
    wait(picks[:1])
    outs += start([pltpu.make_async_copy(picked.at[:, there], p_hbm.at[:, there], osems.at[4])])
    wait(outs)


def pick_columns(tokens, cot, place):
    n = tokens.shape[0]
    return call(
        pick_kernel,
        "pick_columns",
        (place, tokens, cot),
        [((n, 5120), bf16)],
        [pltpu.VMEM((n, 5120), bf16), pltpu.SemaphoreType.DMA((9,)), pltpu.SemaphoreType.DMA((5,))],
    )[0]


def rank_kernel(
    s_ref, t_hbm, tr_hbm, cot_hbm, up_hbm, ups_hbm, g_hbm, whole_hbm, br_hbm,
    whole, cot2, br, flip, tbuf, gbuf, usems, csems, tsems, gsems, osems,
):
    n = t_hbm.shape[0]
    c = s_ref[0]
    first = start(row_copies(up_hbm, ups_hbm, whole, usems, c) + cot_copies(cot_hbm, tr_hbm, cot2, csems))
    ins = []
    for k in range(8):
        there = pl.ds(512 * k, 512)
        ins.append(
            [
                pltpu.make_async_copy(t_hbm.at[:, column(2 * k + c)], tbuf.at[pl.ds(0, n), there], tsems.at[0, k]),
                pltpu.make_async_copy(tr_hbm.at[:, there], tbuf.at[pl.ds(n, n), there], tsems.at[1, k]),
            ]
        )
    wait(first)
    for k in range(3):
        start(ins[k])
    flip[...] = nt(whole[...], cot2[...]).astype(bf16)
    br[...] = nt(cot2[...], whole[...]).astype(bf16)
    outs = start(
        [
            pltpu.make_async_copy(whole, whole_hbm, osems.at[0]),
            pltpu.make_async_copy(br, br_hbm, osems.at[1]),
        ]
    )
    for k in range(8):
        wait(ins[k])
        if k + 3 < 8:
            start(ins[k + 3])
        gbuf[k] = (scale * nn(flip[...], tbuf[:, 512 * k : 512 * k + 512])).astype(bf16)
        outs += start(
            [
                pltpu.make_async_copy(gbuf.at[k, :, pl.ds(128 * j, 128)], g_hbm.at[j, k], gsems.at[j, k])
                for j in range(4)
            ]
        )
    wait(outs)


def rank_partials(tokens, tokens_sib, cot, up, up_sib, place):
    n = tokens.shape[0]
    return call(
        rank_kernel,
        "rank_partials",
        (place, tokens, tokens_sib, cot, up, up_sib),
        [((4, 8, 512, 128), bf16), ((512, 1024), bf16), ((2 * n, 512), bf16)],
        [
            pltpu.VMEM((512, 1024), bf16),
            pltpu.VMEM((2 * n, 1024), bf16),
            pltpu.VMEM((2 * n, 512), bf16),
            pltpu.VMEM((512, 2 * n), bf16),
            pltpu.VMEM((2 * n, 4096), bf16),
            pltpu.VMEM((8, 512, 512), bf16),
            pltpu.SemaphoreType.DMA((2, 8)),
            pltpu.SemaphoreType.DMA((2,)),
            pltpu.SemaphoreType.DMA((2, 8)),
            pltpu.SemaphoreType.DMA((4, 8)),
            pltpu.SemaphoreType.DMA((2,)),
        ],
    )


def low_kernel(s_ref, t_hbm, d_hbm, o_hbm, tbuf, dbuf, total, obuf, tsems, dsems, osem):
    ins = []
    for k in range(8):
        there = pl.ds(1024 * k, 1024)
        ins.append(
            start(
                [
                    pltpu.make_async_copy(d_hbm.at[there], dbuf.at[there], dsems.at[k]),
                    pltpu.make_async_copy(t_hbm.at[:, there], tbuf.at[:, there], tsems.at[k]),
                ]
            )
        )
    for k in range(8):
        wait(ins[k])
        part = nn(tbuf[:, 1024 * k : 1024 * k + 1024], dbuf[1024 * k : 1024 * k + 1024, :])
        total[...] = part if k == 0 else total[...] + part
    obuf[...] = total[...].astype(bf16)
    wait(start([pltpu.make_async_copy(obuf, o_hbm, osem.at[0])]))


def low_rank(tokens, down, place):
    n = tokens.shape[0]
    return call(
        low_kernel,
        "low_rank",
        (place, tokens, down),
        [((n, 512), bf16)],
        [
            pltpu.VMEM((n, 8192), bf16),
            pltpu.VMEM((8192, 512), bf16),
            pltpu.VMEM((n, 512), f32),
            pltpu.VMEM((n, 512), bf16),
            pltpu.SemaphoreType.DMA((8,)),
            pltpu.SemaphoreType.DMA((8,)),
            pltpu.SemaphoreType.DMA((1,)),
        ],
    )[0]


def owner_kernel(
    s_ref, g_hbm, low_hbm, lows_hbm, cot_hbm, tr_hbm, o_hbm, low2, cot2, gbuf, up, obuf, lsems, csems, gsems, osems
):
    n = low_hbm.shape[0]
    c = s_ref[0]
    first = start(
        [
            pltpu.make_async_copy(low_hbm, low2.at[pl.ds(0, n)], lsems.at[0]),
            pltpu.make_async_copy(lows_hbm, low2.at[pl.ds(n, n)], lsems.at[1]),
        ]
        + cot_copies(cot_hbm, tr_hbm, cot2, csems)
    )
    ins = [start([pltpu.make_async_copy(g_hbm.at[:, k], gbuf.at[k], gsems.at[k])]) for k in range(8)]
    wait(first)
    up[...] = (scale * tn(low2[...], cot2[...])).astype(bf16)
    outs = []
    for k in range(8):
        wait(ins[k])
        g = gbuf[k].astype(f32)
        g = ((g[0] + g[1]) + (g[2] + g[3])).astype(bf16)
        rows = up[pl.ds(pl.multiple_of(64 * k + 32 * c, 32), 32), :]
        for zl in range(2):
            obuf[2 * k + zl, :256] = g[256 * zl : 256 * zl + 256]
            for j in range(4):
                cols = 512 * zl + 128 * j
                obuf[2 * k + zl, 256 + 32 * j : 288 + 32 * j] = rows[:, cols : cols + 128]
        there = pl.ds(2 * k, 2)
        outs += start([pltpu.make_async_copy(obuf.at[there], o_hbm.at[there], osems.at[k])])
    wait(outs)


def owner_pieces(g, low, low_sib, cot, tokens_sib, place):
    n = low.shape[0]
    return call(
        owner_kernel,
        "owner_pieces",
        (place, g, low, low_sib, cot, tokens_sib),
        [((16, 384, 128), bf16)],
        [
            pltpu.VMEM((2 * n, 512), bf16),
            pltpu.VMEM((2 * n, 1024), bf16),
            pltpu.VMEM((8, 4, 512, 128), bf16),
            pltpu.VMEM((512, 1024), bf16),
            pltpu.VMEM((16, 384, 128), bf16),
            pltpu.SemaphoreType.DMA((2,)),
            pltpu.SemaphoreType.DMA((2,)),
            pltpu.SemaphoreType.DMA((8,)),
            pltpu.SemaphoreType.DMA((8,)),
        ],
    )[0]


def place_rows(out_ref, own_ref, sib_ref, c):
    n = own_ref.shape[1]
    for j in range(8):
        own, sib = (pl.multiple_of((2 * j + i) * n, n) for i in (c, 1 - c))
        out_ref[pl.ds(own, n), :] = own_ref[j].astype(out_ref.dtype)
        out_ref[pl.ds(sib, n), :] = sib_ref[j].astype(out_ref.dtype)


def merge_kernel(s_ref, m_ref, a_ref, b_ref, bs_ref, o_ref, w_ref, prior):
    place_rows(prior, b_ref, bs_ref, s_ref[0])
    for j in range(4):
        cols = slice(256 * j, 256 * j + 256)
        add = lax.dot_general(
            a_ref[...], prior[:, cols], (((1,), (0,)), ((), ())),
            precision=lax.Precision.HIGHEST, preferred_element_type=f32,
        )
        out = m_ref[:, cols] + scale * add
        o_ref[:, cols] = out
        w_ref[:, cols] = out.astype(bf16)


def merge(master, prev_down, prior, prior_sib, place):
    whole = pl.BlockSpec((512, 1024), lambda i: (0, 0))
    first = pl.BlockSpec((8, 32, 1024), lambda i: (0, 0, 0))
    return pl.pallas_call(
        merge_kernel,
        grid=(1,),
        in_specs=[
            pl.BlockSpec(memory_space=pltpu.SMEM),
            whole,
            pl.BlockSpec((512, 512), lambda i: (0, 0)),
            first,
            first,
        ],
        out_specs=[whole] * 2,
        out_shape=[jax.ShapeDtypeStruct((512, 1024), f32), jax.ShapeDtypeStruct((512, 1024), bf16)],
        scratch_shapes=[pltpu.VMEM((512, 1024), f32)],
        compiler_params=pltpu.CompilerParams(vmem_limit_bytes=VMEM),
        cost_estimate=COST,
        name="merge",
    )(place, master, prev_down, prior, prior_sib)


def main_kernel(at, units, before, added, s_ref, t_hbm, tr_hbm, d_hbm, cot_hbm, br_hbm, *rest):
    n = t_hbm.shape[0]
    w_hbm, rest = rest[:units], rest[units:]
    if added:
        (v_hbm, _), rest = (rest[:2], rest[2]), rest[3:]
    if before:
        r_hbm, rest = rest[0], rest[1:]
    vo_hbm, vs_hbm, x_hbm, o_hbm, cot2, br, tbuf, wbuf, dbuf, xbuf, vbuf, lbuf, rest = *rest[:12], rest[12:]
    csems, tsems, wsems, osems, vsems, rsems = rest

    def span(u):
        return pl.ds(512 * u, 512)

    late = []
    if before:
        late = [pltpu.make_async_copy(r_hbm, lbuf, rsems.at[before])]
    ins, tokens = [], []
    for u in range(units):
        ins.append(
            [
                pltpu.make_async_copy(w_hbm[u], wbuf.at[span(u)], wsems.at[0, u]),
                pltpu.make_async_copy(d_hbm.at[column(s_ref[at + 2 * units + before + u])], dbuf.at[u], wsems.at[1, u]),
            ]
        )
        here = t_hbm.at[:, column(s_ref[at + u])]
        there = tr_hbm.at[:, column(s_ref[at + units + u])]
        tokens.append(pltpu.make_async_copy(here, tbuf.at[pl.ds(0, n), span(u)], tsems.at[0, u]))
        tokens.append(pltpu.make_async_copy(there, tbuf.at[pl.ds(n, n), span(u)], tsems.at[1, u]))
    if added:
        late.append(pltpu.make_async_copy(v_hbm[0], vbuf.at[pl.ds(0, n)], vsems.at[0, 4]))
        late.append(pltpu.make_async_copy(v_hbm[1], vbuf.at[pl.ds(n, n)], vsems.at[1, 4]))
    first = start(cot_copies(cot_hbm, tr_hbm, cot2, csems) + [pltpu.make_async_copy(br_hbm, br, csems.at[2])])
    start(ins[0])
    wait(first)
    outs = []
    for u in range(units):
        wait(ins[u])
        if u + 1 < units:
            start(ins[u + 1])
        else:
            start(late)
        start(tokens[2 * u : 2 * u + 2])
        x = nt(cot2[...], wbuf[512 * u : 512 * u + 512, :]) + scale * nt(br[...], dbuf[u])
        xbuf[u] = x.astype(bf16)
        outs += start(
            [
                pltpu.make_async_copy(xbuf.at[u, pl.ds(0, n)], x_hbm.at[:, column(s_ref[at + u])], osems.at[0, u]),
                pltpu.make_async_copy(xbuf.at[u, pl.ds(n, n)], o_hbm.at[:, span(u)], osems.at[1, u]),
            ]
        )
    wait(late)
    for u in range(before):
        there = x_hbm.at[:, column(s_ref[at + 2 * units + u])]
        outs += start([pltpu.make_async_copy(lbuf.at[:, span(u)], there, rsems.at[u])])
    wait(tokens)
    for j in range(4):
        cols = slice(256 * j, 256 * j + 256)
        there = pl.ds(256 * j, 256)
        part = nn(tbuf[...], wbuf[:, cols])
        vbuf[:, cols] = part + vbuf[:, cols] if added else part
        outs += start(
            [
                pltpu.make_async_copy(vbuf.at[pl.ds(0, n), there], vo_hbm.at[:, there], vsems.at[0, j]),
                pltpu.make_async_copy(vbuf.at[pl.ds(n, n), there], vs_hbm.at[:, there], vsems.at[1, j]),
            ]
        )
    wait(outs)


def main_group(table, at, tokens, tokens_sib, down, cot, br2, blocks, before=0, carry=()):
    n, d = tokens.shape
    units = len(blocks)
    args = [table, tokens, tokens_sib, down, cot, br2, *blocks]
    aliases = {}
    if carry:
        aliases = {len(args) + 2: 2}
        args += list(carry)

    return call(
        functools.partial(main_kernel, at, units, before, bool(carry)),
        "main_group",
        args,
        [((n, 1024), f32), ((n, 1024), f32), ((n, d), bf16), ((n, 512 * units), bf16)],
        [
            pltpu.VMEM((2 * n, 1024), bf16),
            pltpu.VMEM((2 * n, 512), bf16),
            pltpu.VMEM((2 * n, 512 * units), bf16),
            pltpu.VMEM((512 * units, 1024), bf16),
            pltpu.VMEM((units, 512, 512), bf16),
            pltpu.VMEM((units, 2 * n, 512), bf16),
            pltpu.VMEM((2 * n, 1024), f32),
            pltpu.VMEM((n, 512 * max(before, 1)), bf16),
            pltpu.SemaphoreType.DMA((3,)),
            pltpu.SemaphoreType.DMA((2, units)),
            pltpu.SemaphoreType.DMA((2, units)),
            pltpu.SemaphoreType.DMA((2, units)),
            pltpu.SemaphoreType.DMA((2, 5)),
            pltpu.SemaphoreType.DMA((before + 1,)),
        ],
        aliases,
    )


def sum_kernel(in_ref, o_ref):
    total = in_ref[0].astype(f32)
    for k in range(1, 16):
        total = total + in_ref[k].astype(f32)
    down = total[:256].T.astype(bf16)
    up = total[256:].astype(bf16)
    for k in range(8):
        o_ref[k, :128] = down
        for j in range(2):
            o_ref[k, 128 + 32 * j : 160 + 32 * j, :128] = up[64 * j : 64 * j + 32]
            o_ref[k, 128 + 32 * j : 160 + 32 * j, 128:] = up[64 * j + 32 : 64 * j + 64]


def sum_pieces(pieces):
    vm = pl.BlockSpec(memory_space=pltpu.VMEM)
    return pl.pallas_call(
        sum_kernel,
        in_specs=[vm],
        out_specs=vm,
        out_shape=jax.ShapeDtypeStruct((8, 192, 256), bf16),
        compiler_params=pltpu.CompilerParams(vmem_limit_bytes=VMEM),
        cost_estimate=COST,
        name="sum_pieces",
    )(pieces)


def join_kernel(in_ref, down_ref, up_ref):
    for y in range(4):
        for zl in range(2):
            there = slice(256 * zl, 256 * zl + 256)
            down_ref[128 * y : 128 * y + 128, there] = in_ref[2 * y + zl, :128].astype(f32)
    for zl in range(2):
        for j in range(2):
            rows = slice(128 + 32 * j, 160 + 32 * j)
            parts = [in_ref[2 * y + zl, rows].astype(f32) for y in range(4)]
            total = (parts[0] + parts[1]) + (parts[2] + parts[3])
            up_ref[:, 512 * zl + 256 * j : 512 * zl + 256 * j + 256] = total


def join_pieces(pieces):
    vm = pl.BlockSpec(memory_space=pltpu.VMEM)
    return pl.pallas_call(
        join_kernel,
        in_specs=[vm],
        out_specs=[vm, vm],
        out_shape=[jax.ShapeDtypeStruct((512, 512), f32), jax.ShapeDtypeStruct((32, 1024), f32)],
        compiler_params=pltpu.CompilerParams(vmem_limit_bytes=VMEM),
        cost_estimate=COST,
        name="join_pieces",
    )(pieces)


def place_kernel(at, s_ref, r_hbm, rs_hbm, vo_hbm, vr_hbm, low_hbm, up_hbm, x_in, v_hbm, x_hbm, rbuf, vo, vr, low, up, sems, xsems, vsems):
    ins = start([pltpu.make_async_copy(low_hbm, low, sems.at[0]), pltpu.make_async_copy(up_hbm, up, sems.at[1])])
    late = start(
        [
            pltpu.make_async_copy(r_hbm, rbuf.at[:, pl.ds(0, 1024)], sems.at[2]),
            pltpu.make_async_copy(rs_hbm, rbuf.at[:, pl.ds(1024, 2048)], sems.at[5]),
        ]
    )
    ins += start([pltpu.make_async_copy(vo_hbm, vo, sems.at[3]), pltpu.make_async_copy(vr_hbm, vr, sems.at[4])])
    wait(late)
    outs = []
    for u in range(6):
        there = x_hbm.at[:, column(s_ref[at + u])]
        outs += start([pltpu.make_async_copy(rbuf.at[:, pl.ds(512 * u, 512)], there, xsems.at[u])])
    wait(ins)
    for j in range(4):
        cols = slice(256 * j, 256 * j + 256)
        there = pl.ds(256 * j, 256)
        vo[:, cols] = vo[:, cols] + vr[:, cols] + scale * nn(low[...], up[:, cols])
        outs += start([pltpu.make_async_copy(vo.at[:, there], v_hbm.at[:, there], vsems.at[j])])
    wait(outs)


def place_columns(table, at, x, recv, recv_last, vo, vr, low, up):
    n, d = x.shape
    return call(
        functools.partial(place_kernel, at),
        "place_columns",
        (table, recv, recv_last, vo, vr, low, up, x),
        [((n, 1024), f32), ((n, d), bf16)],
        [
            pltpu.VMEM((n, 3072), bf16),
            pltpu.VMEM((n, 1024), f32),
            pltpu.VMEM((n, 1024), f32),
            pltpu.VMEM((n, 512), bf16),
            pltpu.VMEM((512, 1024), bf16),
            pltpu.SemaphoreType.DMA((6,)),
            pltpu.SemaphoreType.DMA((6,)),
            pltpu.SemaphoreType.DMA((4,)),
        ],
        {7: 1},
    )


def finish_kernel(
    at, s_ref, t_hbm, d_hbm, w_hbm, ws_hbm, cot_hbm, br_hbm, vs_hbm, x_in,
    v_hbm, x_hbm, tbuf, wbuf, dbuf, xbuf, cot, br, vs, vbuf, sems, wsems, xsems, vsems,
):
    n = cot.shape[0]
    first = start(
        [
            pltpu.make_async_copy(cot_hbm, cot, sems.at[1]),
            pltpu.make_async_copy(br_hbm.at[pl.ds(0, n)], br, sems.at[2]),
        ]
    )
    ins, rest = [], []
    for i, w in enumerate((w_hbm, ws_hbm)):
        there = pl.ds(512 * i, 512)
        ins.append(
            [
                pltpu.make_async_copy(w, wbuf.at[there], wsems.at[0, i]),
                pltpu.make_async_copy(d_hbm.at[column(s_ref[at + i])], dbuf.at[i], wsems.at[1, i]),
            ]
        )
        rest.append(pltpu.make_async_copy(t_hbm.at[:, column(s_ref[at + i])], tbuf.at[:, there], wsems.at[2, i]))
    rest.append(pltpu.make_async_copy(vs_hbm, vs, sems.at[0]))
    start(ins[0] + ins[1])
    wait(first)
    outs = []
    for i in range(2):
        wait(ins[i])
        if i == 0:
            start(rest)
        x = nt(cot[...], wbuf[512 * i : 512 * i + 512, :]) + scale * nt(br[...], dbuf[i])
        xbuf[i] = x.astype(bf16)
        outs += start([pltpu.make_async_copy(xbuf.at[i], x_hbm.at[:, column(s_ref[at + i])], xsems.at[i])])
    wait(rest)
    for j in range(4):
        cols = slice(256 * j, 256 * j + 256)
        there = pl.ds(256 * j, 256)
        vbuf[:, cols] = (vs[:, cols] + nn(tbuf[...], wbuf[:, cols])).astype(bf16)
        outs += start([pltpu.make_async_copy(vbuf.at[:, there], v_hbm.at[:, there], vsems.at[j])])
    wait(outs)


def finish(table, at, x, tokens, down, w, w_sib, cot, br2, vs):
    n, d = x.shape
    return call(
        functools.partial(finish_kernel, at),
        "finish",
        (table, tokens, down, w, w_sib, cot, br2, vs, x),
        [((n, 1024), bf16), ((n, d), bf16)],
        [
            pltpu.VMEM((n, 1024), bf16),
            pltpu.VMEM((1024, 1024), bf16),
            pltpu.VMEM((2, 512, 512), bf16),
            pltpu.VMEM((2, n, 512), bf16),
            pltpu.VMEM((n, 1024), bf16),
            pltpu.VMEM((n, 512), bf16),
            pltpu.VMEM((n, 1024), f32),
            pltpu.VMEM((n, 1024), bf16),
            pltpu.SemaphoreType.DMA((3,)),
            pltpu.SemaphoreType.DMA((3, 2)),
            pltpu.SemaphoreType.DMA((2,)),
            pltpu.SemaphoreType.DMA((4,)),
        ],
        {8: 1},
    )


def shards(tokens, master, prev_down, prev_up, fresh_down, fresh_up, cot):
    y, zl, zh, x, c = (lax.axis_index(a) for a in AXES)
    bar = lax.optimization_barrier
    place = jnp.stack([c, zh, x])

    def to_owners(v, axes):
        return lax.all_to_all(v, axes, split_axis=0, concat_axis=0)

    def first_step(v):
        return send(v, "xp"), send(v, "xq"), send(v, "z1")

    def second_step(p, q, far):
        return send(p, "xp"), send(far, "xq"), send(p, "z1")

    def first_step(v):
        return send(v, "xp"), send(v, "xq"), send(v, "z1")

    def second_step(p, q, far):
        return send(p, "xp"), send(far, "xq"), send(p, "z1")

    copies, down_half = prepare(fresh_up, fresh_down)
    copies, down_half, place = bar((copies, down_half, place))
    up = to_owners(copies, ("zh", "x"))
    down = lax.all_gather(down_half, ("zh", "x", "c"), axis=0, tiled=True)
    picked = pick_columns(tokens, cot, place)
    prior = jnp.broadcast_to(prev_up[None], (8,) + prev_up.shape)
    up, prior, picked = bar((up, prior, picked))
    tokens_sib = send(picked, "core")
    up_sib = send(up, "core")

    prior = to_owners(prior, ("zh", "x"))
    g, up_rows, br2 = rank_partials(tokens, tokens_sib, cot, up, up_sib, place)
    prior, g = bar((prior, g))
    prior_sib = send(prior, "core")
    g = to_owners(g, ("y",))

    merged, w = merge(master, prev_down, prior, prior_sib, place)
    first = first_step(w)

    def groups_of(core):
        s = 1 - 2 * core
        p, q, r = (x - s) % 4, (x + s) % 4, (x + 2) % 4
        here, there = 4 * zh, 4 * (1 - zh)
        own, two = (here + x)[None], jnp.stack([here + p, here + q])
        four = jnp.stack([there + x, here + r, there + p, there + q])
        return own, two, four, (there + r)[None]

    own = groups_of(c)
    mine = [2 * k + c for k in own]
    sib = [2 * k + 1 - c for k in groups_of(1 - c)]
    parts = [mine[0], own[0], 0 * own[0]]
    parts += [mine[1], own[1], mine[1]]
    parts += [mine[2], own[2], sib[0], mine[2]]
    parts += [sib[1], sib[2], mine[3], sib[3]]
    table = jnp.concatenate(parts).astype(jnp.int32)

    vo, vs, dx, other = main_group(table, 0, tokens, tokens_sib, down_half, cot, br2, [w])
    p, q, far, vo, vs, dx, other = bar(first + (vo, vs, dx, other))
    second = second_step(p, q, far)

    shared = (tokens, tokens_sib, down, cot, br2)
    low = low_rank(tokens, down, place)
    pieces = owner_pieces(g, low, send(low, "core"), cot, tokens_sib, place)
    pieces, p = bar((pieces, p))
    first_sib = send(other, "core")
    part = main_group(table, 3, *shared, [p, q], 0, (vo, vs, dx))
    r, far_q, far_p, part, first_sib = bar(second + (part, first_sib))

    far_r = send(far_q, "xq")
    pieces = to_owners(pieces, ("zh", "x", "zl"))
    vo, vs, dx, other = part
    second_sib = send(other, "core")
    part = main_group(table, 9, *shared, [far, r, far_p, far_q], 1, (vo, vs, dx, first_sib))
    part, pieces, second_sib = bar((part, sum_pieces(pieces), second_sib))

    pieces = to_owners(pieces, ("y", "zl"))
    vo, vs, dx, other = part
    v, dx = place_columns(table, 22, dx, second_sib, send(other, "core"), vo, send(vs, "core"), low, up_rows)
    values, dx = finish(table, 28, dx, tokens, down, far_r, send(far_r, "core"), cot, br2, v)
    pieces, values = bar((pieces, values))
    down_grad, up_grad = join_pieces(pieces)
    return merged, values, dx, down_grad, up_grad


def solution(mesh):
    fine = Mesh(mesh.devices.reshape(SIZES), AXES)
    dp, fsdp = ("y", "zl"), ("zh", "x", "c")
    rows, owned = P(dp + fsdp, None), P(fsdp, None)
    return jax.shard_map(
        shards,
        mesh=fine,
        in_specs=(rows, owned, owned, owned, owned, owned, rows),
        out_specs=(owned, rows, rows, owned, owned),
        check_vma=False,
    )
```

```python
import functools

import jax
import jax.numpy as jnp
import numpy as np
from jax import lax
from jax.experimental import pallas as pl
from jax.experimental.pallas import tpu as pltpu
from jax.sharding import Mesh
from jax.sharding import PartitionSpec as P

scale = 0.25
AXES = ("y", "zl", "zh", "x", "c")
SIZES = (4, 2, 2, 4, 2)
bf16 = jnp.bfloat16
f32 = jnp.float32
VMEM = 32 * 2**20
MOST = 60 * 2**20
COST = pl.CostEstimate(flops=0, bytes_accessed=2**16, transcendentals=0)


def pairs(move):
    out = []
    for i in range(128):
        y, zl, zh, x, c = (int(v) for v in np.unravel_index(i, SIZES))
        x2, y2, z2, c2 = move(x, y, 2 * zh + zl, c)
        z2 %= 4
        j = np.ravel_multi_index((y2 % 4, z2 % 2, z2 // 2, x2 % 4, c2), SIZES)
        out.append((i, int(j)))
    return out


def sg(c):
    return 1 - 2 * c


MOVES = {
    "core": pairs(lambda x, y, z, c: (x, y, z, 1 - c)),
    "xp": pairs(lambda x, y, z, c: (x + sg(c), y, z, c)),
    "xq": pairs(lambda x, y, z, c: (x - sg(c), y, z, c)),
    "z1": pairs(lambda x, y, z, c: (x, y, 3 - z, c)),
}


def send(v, move):
    return lax.ppermute(v, AXES, MOVES[move])


def nt(a, b):
    return lax.dot_general(a, b, (((1,), (1,)), ((), ())), preferred_element_type=f32)


def tn(a, b):
    return lax.dot_general(a, b, (((0,), (0,)), ((), ())), preferred_element_type=f32)


def nn(a, b):
    return lax.dot_general(a, b, (((1,), (0,)), ((), ())), preferred_element_type=f32)


def call(kernel, name, args, out_shape, scratch, aliases={}):
    hbm = pl.BlockSpec(memory_space=pltpu.HBM)
    return pl.pallas_call(
        kernel,
        in_specs=[pl.BlockSpec(memory_space=pltpu.SMEM)] + [hbm] * (len(args) - 1),
        out_specs=[hbm] * len(out_shape),
        out_shape=[jax.ShapeDtypeStruct(*s) for s in out_shape],
        scratch_shapes=scratch,
        input_output_aliases=aliases,
        compiler_params=pltpu.CompilerParams(vmem_limit_bytes=MOST),
        cost_estimate=COST,
        name=name,
    )(*args)


def column(i):
    return pl.ds(pl.multiple_of(i * 512, 512), 512)


def start(copies):
    for cp in copies:
        cp.start()
    return copies


def wait(copies):
    for cp in copies:
        cp.wait()


def row_copies(own_hbm, sib_hbm, out, sems, c):
    n = own_hbm.shape[1]
    copies = []
    for j in range(8):
        own, sib = (pl.ds(pl.multiple_of((2 * j + i) * n, n), n) for i in (c, 1 - c))
        copies.append(pltpu.make_async_copy(own_hbm.at[j], out.at[own], sems.at[0, j]))
        copies.append(pltpu.make_async_copy(sib_hbm.at[j], out.at[sib], sems.at[1, j]))
    return copies


def cot_copies(cot_hbm, tr_hbm, out, sems):
    n = cot_hbm.shape[0]
    return [
        pltpu.make_async_copy(cot_hbm, out.at[pl.ds(0, n)], sems.at[0]),
        pltpu.make_async_copy(tr_hbm.at[:, pl.ds(4096, 1024)], out.at[pl.ds(n, n)], sems.at[1]),
    ]


def prepare_kernel(up_ref, down_ref, o_ref, d_ref):
    up = up_ref[...].astype(bf16)
    for k in range(8):
        o_ref[k] = up
    d_ref[...] = down_ref[...].astype(bf16)


def prepare(up, down):
    vm = pl.BlockSpec(memory_space=pltpu.VMEM)
    return pl.pallas_call(
        prepare_kernel,
        in_specs=[vm, vm],
        out_specs=[vm, vm],
        out_shape=[jax.ShapeDtypeStruct((8,) + up.shape, bf16), jax.ShapeDtypeStruct(down.shape, bf16)],
        cost_estimate=COST,
        name="prepare",
    )(up, down)


def pick_kernel(s_ref, t_hbm, cot_hbm, p_hbm, picked, psems, osems):
    c = s_ref[0]
    picks = start([pltpu.make_async_copy(cot_hbm, picked.at[:, pl.ds(4096, 1024)], psems.at[8])])
    for k in range(8):
        there = picked.at[:, pl.ds(512 * k, 512)]
        picks += start([pltpu.make_async_copy(t_hbm.at[:, column(2 * k + 1 - c)], there, psems.at[k])])
    outs = []
    for k in range(4):
        wait(picks[2 * k + 1 : 2 * k + 3])
        there = pl.ds(1024 * k, 1024)
        outs += start([pltpu.make_async_copy(picked.at[:, there], p_hbm.at[:, there], osems.at[k])])
    there = pl.ds(4096, 1024)
    wait(picks[:1])
    outs += start([pltpu.make_async_copy(picked.at[:, there], p_hbm.at[:, there], osems.at[4])])
    wait(outs)


def pick_columns(tokens, cot, place):
    n = tokens.shape[0]
    return call(
        pick_kernel,
        "pick_columns",
        (place, tokens, cot),
        [((n, 5120), bf16)],
        [pltpu.VMEM((n, 5120), bf16), pltpu.SemaphoreType.DMA((9,)), pltpu.SemaphoreType.DMA((5,))],
    )[0]


def rank_kernel(
    s_ref, t_hbm, tr_hbm, cot_hbm, up_hbm, ups_hbm, g_hbm, whole_hbm, br_hbm,
    whole, cot2, br, flip, tbuf, gbuf, usems, csems, tsems, gsems, osems,
):
    n = t_hbm.shape[0]
    c = s_ref[0]
    first = start(row_copies(up_hbm, ups_hbm, whole, usems, c) + cot_copies(cot_hbm, tr_hbm, cot2, csems))
    ins = []
    for k in range(8):
        there = pl.ds(512 * k, 512)
        ins.append(
            [
                pltpu.make_async_copy(t_hbm.at[:, column(2 * k + c)], tbuf.at[pl.ds(0, n), there], tsems.at[0, k]),
                pltpu.make_async_copy(tr_hbm.at[:, there], tbuf.at[pl.ds(n, n), there], tsems.at[1, k]),
            ]
        )
    wait(first)
    for k in range(3):
        start(ins[k])
    flip[...] = nt(whole[...], cot2[...]).astype(bf16)
    br[...] = nt(cot2[...], whole[...]).astype(bf16)
    outs = start(
        [
            pltpu.make_async_copy(whole, whole_hbm, osems.at[0]),
            pltpu.make_async_copy(br, br_hbm, osems.at[1]),
        ]
    )
    for k in range(8):
        wait(ins[k])
        if k + 3 < 8:
            start(ins[k + 3])
        gbuf[k] = (scale * nn(flip[...], tbuf[:, 512 * k : 512 * k + 512])).astype(bf16)
        outs += start(
            [
                pltpu.make_async_copy(gbuf.at[k, :, pl.ds(128 * j, 128)], g_hbm.at[j, k], gsems.at[j, k])
                for j in range(4)
            ]
        )
    wait(outs)


def rank_partials(tokens, tokens_sib, cot, up, up_sib, place):
    n = tokens.shape[0]
    return call(
        rank_kernel,
        "rank_partials",
        (place, tokens, tokens_sib, cot, up, up_sib),
        [((4, 8, 512, 128), bf16), ((512, 1024), bf16), ((2 * n, 512), bf16)],
        [
            pltpu.VMEM((512, 1024), bf16),
            pltpu.VMEM((2 * n, 1024), bf16),
            pltpu.VMEM((2 * n, 512), bf16),
            pltpu.VMEM((512, 2 * n), bf16),
            pltpu.VMEM((2 * n, 4096), bf16),
            pltpu.VMEM((8, 512, 512), bf16),
            pltpu.SemaphoreType.DMA((2, 8)),
            pltpu.SemaphoreType.DMA((2,)),
            pltpu.SemaphoreType.DMA((2, 8)),
            pltpu.SemaphoreType.DMA((4, 8)),
            pltpu.SemaphoreType.DMA((2,)),
        ],
    )


def low_kernel(s_ref, t_hbm, d_hbm, o_hbm, tbuf, dbuf, total, obuf, tsems, dsems, osem):
    ins = []
    for k in range(8):
        there = pl.ds(1024 * k, 1024)
        ins.append(
            start(
                [
                    pltpu.make_async_copy(d_hbm.at[there], dbuf.at[there], dsems.at[k]),
                    pltpu.make_async_copy(t_hbm.at[:, there], tbuf.at[:, there], tsems.at[k]),
                ]
            )
        )
    for k in range(8):
        wait(ins[k])
        part = nn(tbuf[:, 1024 * k : 1024 * k + 1024], dbuf[1024 * k : 1024 * k + 1024, :])
        total[...] = part if k == 0 else total[...] + part
    obuf[...] = total[...].astype(bf16)
    wait(start([pltpu.make_async_copy(obuf, o_hbm, osem.at[0])]))


def low_rank(tokens, down, place):
    n = tokens.shape[0]
    return call(
        low_kernel,
        "low_rank",
        (place, tokens, down),
        [((n, 512), bf16)],
        [
            pltpu.VMEM((n, 8192), bf16),
            pltpu.VMEM((8192, 512), bf16),
            pltpu.VMEM((n, 512), f32),
            pltpu.VMEM((n, 512), bf16),
            pltpu.SemaphoreType.DMA((8,)),
            pltpu.SemaphoreType.DMA((8,)),
            pltpu.SemaphoreType.DMA((1,)),
        ],
    )[0]


def owner_kernel(
    s_ref, g_hbm, low_hbm, lows_hbm, cot_hbm, tr_hbm, o_hbm, low2, cot2, gbuf, up, obuf, lsems, csems, gsems, osems
):
    n = low_hbm.shape[0]
    c = s_ref[0]
    first = start(
        [
            pltpu.make_async_copy(low_hbm, low2.at[pl.ds(0, n)], lsems.at[0]),
            pltpu.make_async_copy(lows_hbm, low2.at[pl.ds(n, n)], lsems.at[1]),
        ]
        + cot_copies(cot_hbm, tr_hbm, cot2, csems)
    )
    ins = [start([pltpu.make_async_copy(g_hbm.at[:, k], gbuf.at[k], gsems.at[k])]) for k in range(8)]
    wait(first)
    up[...] = (scale * tn(low2[...], cot2[...])).astype(bf16)
    outs = []
    for k in range(8):
        wait(ins[k])
        g = gbuf[k].astype(f32)
        g = ((g[0] + g[1]) + (g[2] + g[3])).astype(bf16)
        rows = up[pl.ds(pl.multiple_of(64 * k + 32 * c, 32), 32), :]
        for zl in range(2):
            obuf[2 * k + zl, :256] = g[256 * zl : 256 * zl + 256]
            for j in range(4):
                cols = 512 * zl + 128 * j
                obuf[2 * k + zl, 256 + 32 * j : 288 + 32 * j] = rows[:, cols : cols + 128]
        there = pl.ds(2 * k, 2)
        outs += start([pltpu.make_async_copy(obuf.at[there], o_hbm.at[there], osems.at[k])])
    wait(outs)


def owner_pieces(g, low, low_sib, cot, tokens_sib, place):
    n = low.shape[0]
    return call(
        owner_kernel,
        "owner_pieces",
        (place, g, low, low_sib, cot, tokens_sib),
        [((16, 384, 128), bf16)],
        [
            pltpu.VMEM((2 * n, 512), bf16),
            pltpu.VMEM((2 * n, 1024), bf16),
            pltpu.VMEM((8, 4, 512, 128), bf16),
            pltpu.VMEM((512, 1024), bf16),
            pltpu.VMEM((16, 384, 128), bf16),
            pltpu.SemaphoreType.DMA((2,)),
            pltpu.SemaphoreType.DMA((2,)),
            pltpu.SemaphoreType.DMA((8,)),
            pltpu.SemaphoreType.DMA((8,)),
        ],
    )[0]


def place_rows(out_ref, own_ref, sib_ref, c):
    n = own_ref.shape[1]
    for j in range(8):
        own, sib = (pl.multiple_of((2 * j + i) * n, n) for i in (c, 1 - c))
        out_ref[pl.ds(own, n), :] = own_ref[j].astype(out_ref.dtype)
        out_ref[pl.ds(sib, n), :] = sib_ref[j].astype(out_ref.dtype)


def merge_kernel(s_ref, m_ref, a_ref, b_ref, bs_ref, o_ref, w_ref, prior):
    place_rows(prior, b_ref, bs_ref, s_ref[0])
    for j in range(4):
        cols = slice(256 * j, 256 * j + 256)
        add = lax.dot_general(
            a_ref[...], prior[:, cols], (((1,), (0,)), ((), ())),
            precision=lax.Precision.HIGHEST, preferred_element_type=f32,
        )
        out = m_ref[:, cols] + scale * add
        o_ref[:, cols] = out
        w_ref[:, cols] = out.astype(bf16)


def merge(master, prev_down, prior, prior_sib, place):
    whole = pl.BlockSpec((512, 1024), lambda i: (0, 0))
    first = pl.BlockSpec((8, 32, 1024), lambda i: (0, 0, 0))
    return pl.pallas_call(
        merge_kernel,
        grid=(1,),
        in_specs=[
            pl.BlockSpec(memory_space=pltpu.SMEM),
            whole,
            pl.BlockSpec((512, 512), lambda i: (0, 0)),
            first,
            first,
        ],
        out_specs=[whole] * 2,
        out_shape=[jax.ShapeDtypeStruct((512, 1024), f32), jax.ShapeDtypeStruct((512, 1024), bf16)],
        scratch_shapes=[pltpu.VMEM((512, 1024), f32)],
        compiler_params=pltpu.CompilerParams(vmem_limit_bytes=VMEM),
        cost_estimate=COST,
        name="merge",
    )(place, master, prev_down, prior, prior_sib)


def main_kernel(at, units, before, added, s_ref, t_hbm, tr_hbm, d_hbm, cot_hbm, br_hbm, *rest):
    n = t_hbm.shape[0]
    w_hbm, rest = rest[:units], rest[units:]
    if added:
        (v_hbm, _), rest = (rest[:2], rest[2]), rest[3:]
    if before:
        r_hbm, rest = rest[0], rest[1:]
    vo_hbm, vs_hbm, x_hbm, o_hbm, cot2, br, tbuf, wbuf, dbuf, xbuf, vbuf, lbuf, rest = *rest[:12], rest[12:]
    csems, tsems, wsems, osems, vsems, rsems = rest

    def span(u):
        return pl.ds(512 * u, 512)

    late = []
    if before:
        late = [pltpu.make_async_copy(r_hbm, lbuf, rsems.at[before])]
    ins, tokens = [], []
    for u in range(units):
        ins.append(
            [
                pltpu.make_async_copy(w_hbm[u], wbuf.at[span(u)], wsems.at[0, u]),
                pltpu.make_async_copy(d_hbm.at[column(s_ref[at + 2 * units + before + u])], dbuf.at[u], wsems.at[1, u]),
            ]
        )
        here = t_hbm.at[:, column(s_ref[at + u])]
        there = tr_hbm.at[:, column(s_ref[at + units + u])]
        tokens.append(pltpu.make_async_copy(here, tbuf.at[pl.ds(0, n), span(u)], tsems.at[0, u]))
        tokens.append(pltpu.make_async_copy(there, tbuf.at[pl.ds(n, n), span(u)], tsems.at[1, u]))
    if added:
        late.append(pltpu.make_async_copy(v_hbm[0], vbuf.at[pl.ds(0, n)], vsems.at[0, 4]))
        late.append(pltpu.make_async_copy(v_hbm[1], vbuf.at[pl.ds(n, n)], vsems.at[1, 4]))
    first = start(cot_copies(cot_hbm, tr_hbm, cot2, csems) + [pltpu.make_async_copy(br_hbm, br, csems.at[2])])
    for u in range(min(units, 2)):
        start(ins[u])
    wait(first)
    outs = []
    for u in range(units):
        wait(ins[u])
        if u + 2 < units:
            start(ins[u + 2])
        if u == 0:
            start(late)
        start(tokens[2 * u : 2 * u + 2])
        x = nt(cot2[...], wbuf[512 * u : 512 * u + 512, :]) + scale * nt(br[...], dbuf[u])
        xbuf[u] = x.astype(bf16)
        outs += start(
            [
                pltpu.make_async_copy(xbuf.at[u, pl.ds(0, n)], x_hbm.at[:, column(s_ref[at + u])], osems.at[0, u]),
                pltpu.make_async_copy(xbuf.at[u, pl.ds(n, n)], o_hbm.at[:, span(u)], osems.at[1, u]),
            ]
        )
    wait(late)
    for u in range(before):
        there = x_hbm.at[:, column(s_ref[at + 2 * units + u])]
        outs += start([pltpu.make_async_copy(lbuf.at[:, span(u)], there, rsems.at[u])])
    wait(tokens)
    for j in range(4):
        cols = slice(256 * j, 256 * j + 256)
        there = pl.ds(256 * j, 256)
        part = nn(tbuf[...], wbuf[:, cols])
        vbuf[:, cols] = part + vbuf[:, cols] if added else part
        outs += start(
            [
                pltpu.make_async_copy(vbuf.at[pl.ds(0, n), there], vo_hbm.at[:, there], vsems.at[0, j]),
                pltpu.make_async_copy(vbuf.at[pl.ds(n, n), there], vs_hbm.at[:, there], vsems.at[1, j]),
            ]
        )
    wait(outs)


def main_group(table, at, tokens, tokens_sib, down, cot, br2, blocks, before=0, carry=()):
    n, d = tokens.shape
    units = len(blocks)
    args = [table, tokens, tokens_sib, down, cot, br2, *blocks]
    aliases = {}
    if carry:
        aliases = {len(args) + 2: 2}
        args += list(carry)

    return call(
        functools.partial(main_kernel, at, units, before, bool(carry)),
        "main_group",
        args,
        [((n, 1024), f32), ((n, 1024), f32), ((n, d), bf16), ((n, 512 * units), bf16)],
        [
            pltpu.VMEM((2 * n, 1024), bf16),
            pltpu.VMEM((2 * n, 512), bf16),
            pltpu.VMEM((2 * n, 512 * units), bf16),
            pltpu.VMEM((512 * units, 1024), bf16),
            pltpu.VMEM((units, 512, 512), bf16),
            pltpu.VMEM((units, 2 * n, 512), bf16),
            pltpu.VMEM((2 * n, 1024), f32),
            pltpu.VMEM((n, 512 * max(before, 1)), bf16),
            pltpu.SemaphoreType.DMA((3,)),
            pltpu.SemaphoreType.DMA((2, units)),
            pltpu.SemaphoreType.DMA((2, units)),
            pltpu.SemaphoreType.DMA((2, units)),
            pltpu.SemaphoreType.DMA((2, 5)),
            pltpu.SemaphoreType.DMA((before + 1,)),
        ],
        aliases,
    )


def sum_kernel(in_ref, o_ref):
    total = in_ref[0].astype(f32)
    for k in range(1, 16):
        total = total + in_ref[k].astype(f32)
    down = total[:256].T.astype(bf16)
    up = total[256:].astype(bf16)
    for k in range(8):
        o_ref[k, :128] = down
        for j in range(2):
            o_ref[k, 128 + 32 * j : 160 + 32 * j, :128] = up[64 * j : 64 * j + 32]
            o_ref[k, 128 + 32 * j : 160 + 32 * j, 128:] = up[64 * j + 32 : 64 * j + 64]


def sum_pieces(pieces):
    vm = pl.BlockSpec(memory_space=pltpu.VMEM)
    return pl.pallas_call(
        sum_kernel,
        in_specs=[vm],
        out_specs=vm,
        out_shape=jax.ShapeDtypeStruct((8, 192, 256), bf16),
        compiler_params=pltpu.CompilerParams(vmem_limit_bytes=VMEM),
        cost_estimate=COST,
        name="sum_pieces",
    )(pieces)


def join_kernel(in_ref, down_ref, up_ref):
    for y in range(4):
        for zl in range(2):
            there = slice(256 * zl, 256 * zl + 256)
            down_ref[128 * y : 128 * y + 128, there] = in_ref[2 * y + zl, :128].astype(f32)
    for zl in range(2):
        for j in range(2):
            rows = slice(128 + 32 * j, 160 + 32 * j)
            parts = [in_ref[2 * y + zl, rows].astype(f32) for y in range(4)]
            total = (parts[0] + parts[1]) + (parts[2] + parts[3])
            up_ref[:, 512 * zl + 256 * j : 512 * zl + 256 * j + 256] = total


def join_pieces(pieces):
    vm = pl.BlockSpec(memory_space=pltpu.VMEM)
    return pl.pallas_call(
        join_kernel,
        in_specs=[vm],
        out_specs=[vm, vm],
        out_shape=[jax.ShapeDtypeStruct((512, 512), f32), jax.ShapeDtypeStruct((32, 1024), f32)],
        compiler_params=pltpu.CompilerParams(vmem_limit_bytes=VMEM),
        cost_estimate=COST,
        name="join_pieces",
    )(pieces)


def place_kernel(at, s_ref, r_hbm, rs_hbm, vo_hbm, vr_hbm, low_hbm, up_hbm, x_in, v_hbm, x_hbm, rbuf, vo, vr, low, up, sems, xsems, vsems):
    ins = start([pltpu.make_async_copy(low_hbm, low, sems.at[0]), pltpu.make_async_copy(up_hbm, up, sems.at[1])])
    late = start(
        [
            pltpu.make_async_copy(r_hbm, rbuf.at[:, pl.ds(0, 1024)], sems.at[2]),
            pltpu.make_async_copy(rs_hbm, rbuf.at[:, pl.ds(1024, 2048)], sems.at[5]),
        ]
    )
    ins += start([pltpu.make_async_copy(vo_hbm, vo, sems.at[3]), pltpu.make_async_copy(vr_hbm, vr, sems.at[4])])
    wait(late)
    outs = []
    for u in range(6):
        there = x_hbm.at[:, column(s_ref[at + u])]
        outs += start([pltpu.make_async_copy(rbuf.at[:, pl.ds(512 * u, 512)], there, xsems.at[u])])
    wait(ins)
    for j in range(4):
        cols = slice(256 * j, 256 * j + 256)
        there = pl.ds(256 * j, 256)
        vo[:, cols] = vo[:, cols] + vr[:, cols] + scale * nn(low[...], up[:, cols])
        outs += start([pltpu.make_async_copy(vo.at[:, there], v_hbm.at[:, there], vsems.at[j])])
    wait(outs)


def place_columns(table, at, x, recv, recv_last, vo, vr, low, up):
    n, d = x.shape
    return call(
        functools.partial(place_kernel, at),
        "place_columns",
        (table, recv, recv_last, vo, vr, low, up, x),
        [((n, 1024), f32), ((n, d), bf16)],
        [
            pltpu.VMEM((n, 3072), bf16),
            pltpu.VMEM((n, 1024), f32),
            pltpu.VMEM((n, 1024), f32),
            pltpu.VMEM((n, 512), bf16),
            pltpu.VMEM((512, 1024), bf16),
            pltpu.SemaphoreType.DMA((6,)),
            pltpu.SemaphoreType.DMA((6,)),
            pltpu.SemaphoreType.DMA((4,)),
        ],
        {7: 1},
    )


def finish_kernel(
    at, s_ref, t_hbm, d_hbm, w_hbm, ws_hbm, cot_hbm, br_hbm, vs_hbm, x_in,
    v_hbm, x_hbm, tbuf, wbuf, dbuf, xbuf, cot, br, vs, vbuf, sems, wsems, xsems, vsems,
):
    n = cot.shape[0]
    first = start(
        [
            pltpu.make_async_copy(cot_hbm, cot, sems.at[1]),
            pltpu.make_async_copy(br_hbm.at[pl.ds(0, n)], br, sems.at[2]),
        ]
    )
    ins, rest = [], []
    for i, w in enumerate((w_hbm, ws_hbm)):
        there = pl.ds(512 * i, 512)
        ins.append(
            [
                pltpu.make_async_copy(w, wbuf.at[there], wsems.at[0, i]),
                pltpu.make_async_copy(d_hbm.at[column(s_ref[at + i])], dbuf.at[i], wsems.at[1, i]),
            ]
        )
        rest.append(pltpu.make_async_copy(t_hbm.at[:, column(s_ref[at + i])], tbuf.at[:, there], wsems.at[2, i]))
    rest.append(pltpu.make_async_copy(vs_hbm, vs, sems.at[0]))
    start(ins[0] + ins[1])
    wait(first)
    outs = []
    for i in range(2):
        wait(ins[i])
        if i == 0:
            start(rest)
        x = nt(cot[...], wbuf[512 * i : 512 * i + 512, :]) + scale * nt(br[...], dbuf[i])
        xbuf[i] = x.astype(bf16)
        outs += start([pltpu.make_async_copy(xbuf.at[i], x_hbm.at[:, column(s_ref[at + i])], xsems.at[i])])
    wait(rest)
    for j in range(4):
        cols = slice(256 * j, 256 * j + 256)
        there = pl.ds(256 * j, 256)
        vbuf[:, cols] = (vs[:, cols] + nn(tbuf[...], wbuf[:, cols])).astype(bf16)
        outs += start([pltpu.make_async_copy(vbuf.at[:, there], v_hbm.at[:, there], vsems.at[j])])
    wait(outs)


def finish(table, at, x, tokens, down, w, w_sib, cot, br2, vs):
    n, d = x.shape
    return call(
        functools.partial(finish_kernel, at),
        "finish",
        (table, tokens, down, w, w_sib, cot, br2, vs, x),
        [((n, 1024), bf16), ((n, d), bf16)],
        [
            pltpu.VMEM((n, 1024), bf16),
            pltpu.VMEM((1024, 1024), bf16),
            pltpu.VMEM((2, 512, 512), bf16),
            pltpu.VMEM((2, n, 512), bf16),
            pltpu.VMEM((n, 1024), bf16),
            pltpu.VMEM((n, 512), bf16),
            pltpu.VMEM((n, 1024), f32),
            pltpu.VMEM((n, 1024), bf16),
            pltpu.SemaphoreType.DMA((3,)),
            pltpu.SemaphoreType.DMA((3, 2)),
            pltpu.SemaphoreType.DMA((2,)),
            pltpu.SemaphoreType.DMA((4,)),
        ],
        {8: 1},
    )


def shards(tokens, master, prev_down, prev_up, fresh_down, fresh_up, cot):
    y, zl, zh, x, c = (lax.axis_index(a) for a in AXES)
    bar = lax.optimization_barrier
    place = jnp.stack([c, zh, x])

    def to_owners(v, axes):
        return lax.all_to_all(v, axes, split_axis=0, concat_axis=0)

    def first_step(v):
        return send(v, "xp"), send(v, "xq"), send(v, "z1")

    def second_step(p, q, far):
        return send(p, "xp"), send(far, "xq"), send(p, "z1")

    def first_step(v):
        return send(v, "xp"), send(v, "xq"), send(v, "z1")

    def second_step(p, q, far):
        return send(p, "xp"), send(far, "xq"), send(p, "z1")

    copies, down_half = prepare(fresh_up, fresh_down)
    copies, down_half, place = bar((copies, down_half, place))
    up = to_owners(copies, ("zh", "x"))
    down = lax.all_gather(down_half, ("zh", "x", "c"), axis=0, tiled=True)
    picked = pick_columns(tokens, cot, place)
    prior = jnp.broadcast_to(prev_up[None], (8,) + prev_up.shape)
    up, prior, picked = bar((up, prior, picked))
    tokens_sib = send(picked, "core")
    up_sib = send(up, "core")

    prior = to_owners(prior, ("zh", "x"))
    g, up_rows, br2 = rank_partials(tokens, tokens_sib, cot, up, up_sib, place)
    prior, g = bar((prior, g))
    prior_sib = send(prior, "core")
    g = to_owners(g, ("y",))

    merged, w = merge(master, prev_down, prior, prior_sib, place)
    first = first_step(w)

    def groups_of(core):
        s = 1 - 2 * core
        p, q, r = (x - s) % 4, (x + s) % 4, (x + 2) % 4
        here, there = 4 * zh, 4 * (1 - zh)
        own, two = (here + x)[None], jnp.stack([here + p, here + q])
        four = jnp.stack([there + x, here + r, there + p, there + q])
        return own, two, four, (there + r)[None]

    own = groups_of(c)
    mine = [2 * k + c for k in own]
    sib = [2 * k + 1 - c for k in groups_of(1 - c)]
    parts = [mine[0], own[0], 0 * own[0]]
    parts += [mine[1], own[1], mine[1]]
    parts += [mine[2], own[2], sib[0], mine[2]]
    parts += [sib[1], sib[2], mine[3], sib[3]]
    table = jnp.concatenate(parts).astype(jnp.int32)

    vo, vs, dx, other = main_group(table, 0, tokens, tokens_sib, down_half, cot, br2, [w])
    p, q, far, vo, vs, dx, other = bar(first + (vo, vs, dx, other))
    second = second_step(p, q, far)

    shared = (tokens, tokens_sib, down, cot, br2)
    low = low_rank(tokens, down, place)
    pieces = owner_pieces(g, low, send(low, "core"), cot, tokens_sib, place)
    pieces, p = bar((pieces, p))
    first_sib = send(other, "core")
    part = main_group(table, 3, *shared, [p, q], 0, (vo, vs, dx))
    r, far_q, far_p, part, first_sib = bar(second + (part, first_sib))

    far_r = send(far_q, "xq")
    pieces = to_owners(pieces, ("zh", "x", "zl"))
    vo, vs, dx, other = part
    second_sib = send(other, "core")
    part = main_group(table, 9, *shared, [far, r, far_p, far_q], 1, (vo, vs, dx, first_sib))
    part, pieces, second_sib = bar((part, sum_pieces(pieces), second_sib))

    pieces = to_owners(pieces, ("y", "zl"))
    vo, vs, dx, other = part
    v, dx = place_columns(table, 22, dx, second_sib, send(other, "core"), vo, send(vs, "core"), low, up_rows)
    values, dx = finish(table, 28, dx, tokens, down, far_r, send(far_r, "core"), cot, br2, v)
    pieces, values = bar((pieces, values))
    down_grad, up_grad = join_pieces(pieces)
    return merged, values, dx, down_grad, up_grad


def solution(mesh):
    fine = Mesh(mesh.devices.reshape(SIZES), AXES)
    dp, fsdp = ("y", "zl"), ("zh", "x", "c")
    rows, owned = P(dp + fsdp, None), P(fsdp, None)
    return jax.shard_map(
        shards,
        mesh=fine,
        in_specs=(rows, owned, owned, owned, owned, owned, rows),
        out_specs=(owned, rows, rows, owned, owned),
        check_vma=False,
    )
```
